512 devices in a mesh: dp: 32 (over y, x, core), query: 16 (over z).
Axes of the slice: x: 4, y: 4, z: 16, core: 2. Of those that a mesh axis runs over, the one named last changes fastest.
Arguments:
- hidden_acts: bfloat16 [65536, 14336], P('dp', 'query'), may hold values from -40 to 40
- out_grads: bfloat16 [65536, 4096], P('dp', 'query'), may hold values from -40 to 40
- proj_in: bfloat16 [14336, 32], P('query')
- proj_out: bfloat16 [4096, 32], P('query')
- query_codes: float32 [1024, 1024], P('query'), may hold values from -6 to 6
Outputs:
- scores: float32 [65536, 1024], P(('dp', 'query'))
The draws below stay inside these ranges and needn't reach their ends.
All inputs are finite; a program needn't handle non-finite values.
Results may differ from the reference program's by a relative error of at most 0.0003.
Values sent between devices are 32-bit elements; how exact they have to be, the bound alone decides.
A program may use at most 64 MiB of HBM per device.

```python
import jax
import jax.numpy as jnp
from jax import lax

D = 4096
FF = 14336
R = 32
QUERIES = 1024
TOKENS = 65536


def mixed_columns(entries, key_scale, key_shared, spread):
    matrix_rows = entries.shape[0]
    column_scale = jnp.exp(jax.random.uniform(key_scale, (1, entries.shape[1]), jnp.float32, 0.0, jnp.log(spread)))
    shared = jnp.clip(jax.random.normal(key_shared, (matrix_rows, 1), jnp.float32), -6.0, 6.0)
    return (entries + 0.6 * shared) * column_scale / jnp.sqrt(jnp.float32(matrix_rows))


def draw_hidden_acts(key, part):
    key = jax.random.fold_in(key, 11)
    first = jax.random.fold_in(key, 0)
    ramp = (3.0 ** (jnp.arange(TOKENS, dtype=jnp.float32) / TOKENS))[:, None]
    base = jnp.clip(jax.random.normal(first, (TOKENS, FF), jnp.float32), -6.0, 6.0)
    return (base * ramp).astype(jnp.bfloat16)


def draw_out_grads(key, part):
    key = jax.random.fold_in(key, 12)
    first = jax.random.fold_in(key, 0)
    ramp = (3.0 ** (jnp.arange(TOKENS, dtype=jnp.float32) / TOKENS))[:, None]
    base = jnp.clip(jax.random.normal(first, (TOKENS, D), jnp.float32), -6.0, 6.0)
    return (base * ramp).astype(jnp.bfloat16)


def draw_proj_in(key, part):
    key = jax.random.fold_in(key, 13)
    first, second, third = jax.random.split(key, 3)
    entries = jnp.clip(jax.random.normal(first, (FF, R), jnp.float32), -6.0, 6.0)
    return mixed_columns(entries, second, third, 10.0).astype(jnp.bfloat16)


def draw_proj_out(key, part):
    key = jax.random.fold_in(key, 14)
    first, second, third = jax.random.split(key, 3)
    entries = jnp.clip(jax.random.normal(first, (D, R), jnp.float32), -6.0, 6.0)
    return mixed_columns(entries, second, third, 10.0).astype(jnp.bfloat16)


def level_of(key, shape, cuts, least, high):
    gain, own = 1.0, jax.random.fold_in(key, 6)
    for position, parts in cuts:
        draws = jnp.exp(jax.random.uniform(jax.random.fold_in(own, position), (parts,), jnp.float32, least / len(cuts), high / len(cuts)))
        gain = gain * jnp.repeat(draws, shape[position] // parts).reshape([-1 if axis == position else 1 for axis in range(len(shape))])
    return gain


def noise(own_key, shape, deviation, most, cuts=(), kind=jnp.bfloat16):
    values = jax.random.normal(own_key, shape, jnp.float32) * deviation
    if len(cuts) > 0:
        values = level_of(own_key, shape, cuts, -0.22, 0.18) * values
    return jnp.clip(values, min=-most, max=most).astype(kind)


def setup_inputs(seed: int = 0) -> dict:
    key_list = jax.random.split(jax.random.key(seed), 6)
    return {
        "hidden_acts": draw_hidden_acts(jax.random.fold_in(key_list[5], 71), 0),
        "out_grads": draw_out_grads(jax.random.fold_in(key_list[5], 71), 0),
        "proj_in": draw_proj_in(jax.random.fold_in(key_list[5], 71), 0),
        "proj_out": draw_proj_out(jax.random.fold_in(key_list[5], 71), 0),
        "query_codes": noise(key_list[4], (QUERIES, R * R), 1.0, 6.0, ((0, 16),), jnp.float32),
    }


damping = 0.1

def right_solve(factor, matrix):
    halfway = lax.linalg.triangular_solve(factor, matrix, left_side=False, lower=True, transpose_a=True)
    return lax.linalg.triangular_solve(factor, halfway, left_side=False, lower=True, transpose_a=False)

def prepare(query_block, low_in, low_out):
    code_count = query_block.shape[0]
    code_width = low_in.shape[0]
    blocks = query_block.reshape(code_count * code_width, code_width)
    right_done = right_solve(low_in, blocks).reshape(code_count, code_width, code_width)
    flipped = jnp.swapaxes(right_done, 1, 2).reshape(code_count * code_width, code_width)
    both_done = right_solve(low_out, flipped).reshape(code_count, code_width, code_width)
    return jnp.swapaxes(both_done, 1, 2).reshape(code_count, code_width * code_width)

def gram(matrix):
    return jnp.dot(matrix.T.astype(jnp.float32), matrix.astype(jnp.float32), precision=lax.Precision.HIGHEST, preferred_element_type=jnp.float32)

def reference(hidden_acts, out_grads, proj_in, proj_out, query_codes):
    acts_proj = jnp.dot(hidden_acts.astype(jnp.float32), proj_in.astype(jnp.float32), preferred_element_type=jnp.float32)
    grads_proj = jnp.dot(out_grads.astype(jnp.float32), proj_out.astype(jnp.float32), preferred_element_type=jnp.float32)
    identity = jnp.eye(R, dtype=jnp.float32)
    fisher_in = gram(acts_proj) / TOKENS + damping * identity
    fisher_out = gram(grads_proj) / TOKENS + damping * identity
    low_in = jnp.linalg.cholesky(fisher_in)
    low_out = jnp.linalg.cholesky(fisher_out)
    prepared = prepare(query_codes, low_in, low_out)
    token_codes = (grads_proj[:, :, None] * acts_proj[:, None, :]).reshape(TOKENS, R * R)
    scores = lax.dot_general(token_codes.astype(jnp.float32), prepared.astype(jnp.float32), (((1,), (1,)), ((), ())), precision=lax.Precision.HIGHEST, preferred_element_type=jnp.float32)
    return scores / R
```

```python
import jax
import jax.numpy as jnp
from jax import lax
from jax.experimental import pallas as pl
from jax.experimental.pallas import tpu as pltpu
from jax.sharding import PartitionSpec as P

damping = 0.1
MESH = pl.DeviceIdType.MESH
HIGHEST = lax.Precision.HIGHEST
f32 = jnp.float32
bf16 = jnp.bfloat16


def dot_nt(a, b, precision=None):
    return lax.dot_general(
        a, b, (((1,), (1,)), ((), ())), precision=precision, preferred_element_type=f32
    )


def dot_nn(a, b, precision=None):
    return lax.dot_general(
        a, b, (((1,), (0,)), ((), ())), precision=precision, preferred_element_type=f32
    )


def dot_tn(a, b, precision=None):
    return lax.dot_general(
        a, b, (((0,), (0,)), ((), ())), precision=precision, preferred_element_type=f32
    )


def iota(shape, axis):
    return lax.broadcasted_iota(jnp.int32, shape, axis)


def tile_lanes(x, start):
    lane = iota(x.shape, 1)
    kept = jnp.where((lane >= start) & (lane < start + 32), x, 0.0)
    twice = kept + pltpu.roll(kept, 32, 1)
    return twice + pltpu.roll(twice, 64, 1)


def pack(square):
    lane = iota((8, 128), 1) // 32
    tile = square[0:8]
    for k in range(1, 4):
        tile = jnp.where(lane == k, square[8 * k : 8 * k + 8], tile)
    return tile


def unpack(tile):
    rows = [tile] + [pltpu.roll(tile, 128 - 32 * k, 1) for k in range(1, 4)]
    return jnp.concatenate(rows, axis=0)


def inverse(matrix):
    lane = iota((32, 128), 1)
    row_id = iota((32, 128), 0)
    for k in range(32):
        pivot = 1.0 / matrix[k : k + 1, k : k + 1]
        row = jnp.where(lane[0:1] == k, 1.0, matrix[k : k + 1, :]) * pivot
        column = jnp.where(row_id == k, -1.0, matrix[:, k : k + 1])
        base = jnp.where((lane == k) | (row_id == k), 0.0, matrix)
        matrix = base - column * row
    return matrix


def kernel(
    tokens, hid, grd, wi, wo, codes, out,
    hbuf, gbuf, wip, wop, part, from_left, from_right, eighth, second, third,
    fsend, fpair, ftile, fz, zsum, fp, minv, mpair, q, qhi, qlo, expand, chi, clo,
    load_sem, qload_sem, rs_send, rs_recv, f_send, f_recv,
    qz_send, qz_recv, qp_send, qp_recv, qc_send, qc_recv,
):
    dp = lax.axis_index("dp")
    z = lax.axis_index("query")
    core = lax.rem(dp, 2)
    sibling = dp + 1 - 2 * core

    def at_z(offset):
        return lax.rem(z + offset + 16, 16)

    def chip(i):
        return lax.rem(dp + 2 * i, 32)

    def remote(src, dst, ss, rs, device):
        return pltpu.make_async_remote_copy(
            src_ref=src, dst_ref=dst, send_sem=ss, recv_sem=rs,
            device_id=device, device_id_type=MESH,
        )

    loads = []
    for g in range(4):
        rows = pl.ds(512 * g, 512)
        loads.append((
            pltpu.make_async_copy(hid.at[rows, :], hbuf.at[rows, :], load_sem.at[g, 0]),
            pltpu.make_async_copy(grd.at[rows, :], gbuf.at[rows, :], load_sem.at[g, 1]),
        ))
        loads[-1][0].start()
        loads[-1][1].start()

    def q_rows(which):
        return pl.ds(pl.multiple_of((which // 4) * 8, 8), 8)

    def q_lanes(which):
        return pl.ds(pl.multiple_of(lax.rem(which, 4) * 256, 256), 256)

    own_q = pltpu.make_async_copy(
        codes.at[q_rows(dp), q_lanes(dp)], q.at[z, q_rows(dp), q_lanes(dp)], qload_sem
    )
    own_q.start()

    barrier = pltpu.get_barrier_semaphore()

    def hello_z(i, carry):
        pl.semaphore_signal(barrier, inc=1, device_id=(dp, at_z(i)), device_id_type=MESH)
        return carry

    def hello_chip(i, carry):
        pl.semaphore_signal(barrier, inc=1, device_id=(chip(i), z), device_id_type=MESH)
        return carry

    lax.fori_loop(1, 16, hello_z, 0)
    lax.fori_loop(1, 16, hello_chip, 0)
    pl.semaphore_signal(barrier, inc=1, device_id=(sibling, z), device_id_type=MESH)

    wip[...] = jnp.zeros_like(wip)
    wop[...] = jnp.zeros_like(wop)
    wip[0, 0:32, :] = wi[...]
    wip[1, 64:96, :] = wi[...]
    wop[0, 32:64, :] = wo[...]
    wop[1, 96:128, :] = wo[...]
    for g in range(4):
        loads[g][0].wait()
        loads[g][1].wait()
        total = None
        for half in range(2):
            starts = [512 * g + 128 * j + 64 * half for j in range(4)]
            h = jnp.concatenate([hbuf[s : s + 64, :] for s in starts], axis=0)
            o = jnp.concatenate([gbuf[s : s + 64, :] for s in starts], axis=0)
            term = dot_nt(h, wip[half]) + dot_nt(o, wop[half])
            total = term if total is None else total + term
        part[4 * g : 4 * g + 4] = total.reshape(4, 64, 128)

    expand[...] = jnp.where(
        iota((128, 1024), 1) // 32 == iota((128, 1024), 0), 1.0, 0.0
    ).astype(bf16)

    own_q.wait()
    pl.semaphore_wait(barrier, 31)

    stage1 = []
    for m in (2, -2, 1, -1, 0):
        i = m + 2
        right = remote(part.at[at_z(3 * m + 1)], from_left.at[i],
                       rs_send.at[i], rs_recv.at[i], (dp, at_z(1)))
        left = remote(part.at[at_z(3 * m - 1)], from_right.at[i],
                      rs_send.at[5 + i], rs_recv.at[5 + i], (dp, at_z(-1)))
        right.start()
        left.start()
        stage1 += [right, left]
        if abs(m) == 2:
            s = 0 if m == 2 else 1
            far = remote(part.at[at_z(8), pl.ds(32 * s, 32), :], eighth.at[s],
                         rs_send.at[10 + s], rs_recv.at[10 + s],
                         (dp, at_z(2 if m == 2 else -2)))
            far.start()
            stage1.append(far)
    hub2r, hub2l, far_up, hub_2r, hub_2l, far_down, hub1r, hub1l, hub_1r, hub_1l, hub0r, hub0l = stage1

    def send_qz(i, carry):
        remote(q.at[z, q_rows(dp), q_lanes(dp)], q.at[z, q_rows(dp), q_lanes(dp)],
               qz_send.at[i], qz_recv.at[i], (dp, at_z(i))).start()
        return carry

    lax.fori_loop(1, 16, send_qz, 0)

    hub2r.wait_recv()
    hub2l.wait_recv()
    far_up.wait_recv()
    part[at_z(6)] = part[at_z(6)] + from_left[4] + from_right[4]
    part[at_z(6), 0:32, :] = part[at_z(6), 0:32, :] + eighth[0]
    up2 = remote(part.at[at_z(6)], second.at[0], rs_send.at[12], rs_recv.at[12], (dp, at_z(3)))
    up2.start()
    hub_2r.wait_recv()
    hub_2l.wait_recv()
    far_down.wait_recv()
    part[at_z(-6)] = part[at_z(-6)] + from_left[0] + from_right[0]
    part[at_z(-6), 32:64, :] = part[at_z(-6), 32:64, :] + eighth[1]
    down2 = remote(part.at[at_z(-6)], second.at[1], rs_send.at[13], rs_recv.at[13], (dp, at_z(-3)))
    down2.start()

    hub1r.wait_recv()
    hub1l.wait_recv()
    hub_1r.wait_recv()
    hub_1l.wait_recv()
    up = part[at_z(3)] + from_left[3] + from_right[3]
    down = part[at_z(-3)] + from_left[1] + from_right[1]
    hub0r.wait_recv()
    hub0l.wait_recv()
    mine = part[z] + from_left[2] + from_right[2]

    up2.wait_recv()
    part[at_z(3)] = up + second[0]
    up3 = remote(part.at[at_z(3)], third.at[0], rs_send.at[14], rs_recv.at[14], (dp, at_z(3)))
    up3.start()
    down2.wait_recv()
    part[at_z(-3)] = down + second[1]
    down3 = remote(part.at[at_z(-3)], third.at[1], rs_send.at[15], rs_recv.at[15], (dp, at_z(-3)))
    down3.start()

    def wait_qz(i, carry):
        remote(q.at[z, q_rows(dp), q_lanes(dp)], q.at[at_z(-i), q_rows(dp), q_lanes(dp)],
               qz_send.at[i], qz_recv.at[i], (dp, at_z(i))).wait()
        return carry

    lax.fori_loop(1, 16, wait_qz, 0)

    def q_block(which):
        return q.at[:, q_rows(which), q_lanes(which)]

    def send_qp(i, carry):
        remote(q_block(dp), q_block(dp), qp_send.at[i], qp_recv.at[i], (chip(i), z)).start()
        return carry

    lax.fori_loop(1, 16, send_qp, 0)

    up3.wait_recv()
    down3.wait_recv()
    x = mine + third[0] + third[1]

    acts4 = jnp.concatenate([tile_lanes(x, 0), tile_lanes(x, 64)], axis=0)
    grads4 = jnp.concatenate([tile_lanes(x, 32), tile_lanes(x, 96)], axis=0)
    fin = pack(dot_tn(acts4, acts4, HIGHEST)[0:32])
    fout = pack(dot_tn(grads4, grads4, HIGHEST)[0:32])
    first_core = core == 0
    fsend[...] = jnp.where(first_core, fout, fin)
    pair = remote(fsend, fpair, f_send.at[0], f_recv.at[0], (sibling, z))
    pair.start()
    keep = jnp.where(first_core, fin, fout)
    pair.wait_recv()
    ftile[...] = keep + fpair[...]

    def send_fz(i, carry):
        j = lax.rem(i + 7, 15) + 1
        remote(ftile, fz.at[j], f_send.at[j], f_recv.at[j], (dp, at_z(j))).start()
        return carry

    lax.fori_loop(0, 15, send_fz, 0)

    def wait_fz(i, total):
        remote(ftile, fz.at[i], f_send.at[i], f_recv.at[i], (dp, at_z(i))).wait_recv()
        return total + fz[i]

    zsum[...] = lax.fori_loop(1, 16, wait_fz, ftile[...])

    def send_fp(i, carry):
        remote(zsum, fp.at[i], f_send.at[15 + i], f_recv.at[15 + i], (chip(i), z)).start()
        return carry

    lax.fori_loop(1, 16, send_fp, 0)

    def wait_fp(i, total):
        remote(zsum, fp.at[i], f_send.at[15 + i], f_recv.at[15 + i], (chip(i), z)).wait_recv()
        return total + fp[i]

    fisher = unpack(lax.fori_loop(1, 16, wait_fp, zsum[...]))
    eye = iota((32, 128), 0) == iota((32, 128), 1)
    fisher = fisher / tokens + jnp.where(eye, damping, 0.0)
    minv[...] = inverse(jnp.where(iota((32, 128), 1) < 32, fisher, 0.0))
    swap = remote(minv, mpair, f_send.at[31], f_recv.at[31], (sibling, z))
    swap.start()

    def q_to_core(i, carry):
        which = chip(-i + 16)
        @pl.when(i > 0)
        def _():
            remote(q_block(dp), q_block(which), qp_send.at[i], qp_recv.at[i], (chip(i), z)).wait()
        remote(q_block(which), q_block(which), qc_send.at[i], qc_recv.at[i], (sibling, z)).start()
        return carry

    lax.fori_loop(0, 16, q_to_core, 0)

    def q_from_core(i, carry):
        mate = lax.rem(sibling + 32 - 2 * i, 32)
        remote(q_block(chip(-i + 16)), q_block(mate), qc_send.at[i], qc_recv.at[i], (sibling, z)).wait()
        return carry

    lax.fori_loop(0, 16, q_from_core, 0)

    def split_q(i, carry):
        rows = pl.ds(pl.multiple_of(i * 64, 64), 64)
        block = q[i]
        high = block.astype(bf16)
        qhi[rows, :] = high
        qlo[rows, :] = (block - high.astype(f32)).astype(bf16)
        return carry

    lax.fori_loop(0, 16, split_q, 0)

    swap.wait_recv()
    mine_inv, other_inv = minv[...], mpair[...]
    inv_in = tile_lanes(jnp.where(first_core, mine_inv, other_inv), 0)
    inv_out = jnp.where(first_core, other_inv, mine_inv)
    zero = jnp.zeros((32, 128), f32)
    weights = jnp.concatenate([
        jnp.concatenate([inv_in, zero, zero, zero], axis=0),
        jnp.concatenate([zero, zero, inv_in, zero], axis=0),
        jnp.concatenate([zero, inv_out, zero, zero], axis=0),
        jnp.concatenate([zero, zero, zero, inv_out], axis=0),
    ], axis=1)
    ready = dot_nn(x, weights, HIGHEST)
    acts_ready = jnp.concatenate([ready[:, 0:128], ready[:, 128:256]], axis=0)
    grads_ready = jnp.concatenate([ready[:, 256:384], ready[:, 384:512]], axis=0) * (1.0 / 32.0)
    grads_high = grads_ready.astype(bf16)
    grads_low = (grads_ready - grads_high.astype(f32)).astype(bf16)
    for k in range(8):
        lanes = slice(128 * k, 128 * k + 128)
        wide = dot_nn(grads_high, expand[:, lanes]) + dot_nn(grads_low, expand[:, lanes])
        code = wide * acts_ready
        high = code.astype(bf16)
        chi[:, lanes] = high
        clo[:, lanes] = (code - high.astype(f32)).astype(bf16)

    def score(i, carry):
        rows = pl.ds(pl.multiple_of(i * 256, 256), 256)
        high = qhi[rows, :]
        out[:, rows] = (
            dot_nt(chi[...], high) + dot_nt(clo[...], high) + dot_nt(chi[...], qlo[rows, :])
        )
        return carry

    lax.fori_loop(0, 4, score, 0)

    for copy in stage1 + [up2, down2, up3, down3, pair, swap]:
        copy.wait_send()

    def sent(i, carry):
        remote(ftile, fz.at[i], f_send.at[i], f_recv.at[i], (dp, at_z(i))).wait_send()
        remote(zsum, fp.at[i], f_send.at[15 + i], f_recv.at[15 + i], (chip(i), z)).wait_send()
        return carry

    lax.fori_loop(1, 16, sent, 0)


def body(hidden_acts, out_grads, proj_in, proj_out, query_codes):
    tokens = float(hidden_acts.shape[0] * lax.axis_size("dp"))
    vmem = pl.BlockSpec(memory_space=pltpu.VMEM)
    any_space = pl.BlockSpec(memory_space=pl.ANY)
    dma = pltpu.SemaphoreType.DMA

    def call(*refs):
        kernel(tokens, *refs)

    return pl.pallas_call(
        call,
        out_shape=jax.ShapeDtypeStruct((128, 1024), f32),
        in_specs=[any_space, any_space, vmem, vmem, any_space],
        out_specs=vmem,
        scratch_shapes=[
            pltpu.VMEM((2048, 896), bf16),
            pltpu.VMEM((2048, 256), bf16),
            pltpu.VMEM((2, 128, 896), bf16),
            pltpu.VMEM((2, 128, 256), bf16),
            pltpu.VMEM((16, 64, 128), f32),
            pltpu.VMEM((5, 64, 128), f32),
            pltpu.VMEM((5, 64, 128), f32),
            pltpu.VMEM((2, 32, 128), f32),
            pltpu.VMEM((2, 64, 128), f32),
            pltpu.VMEM((2, 64, 128), f32),
            pltpu.VMEM((8, 128), f32),
            pltpu.VMEM((8, 128), f32),
            pltpu.VMEM((8, 128), f32),
            pltpu.VMEM((16, 8, 128), f32),
            pltpu.VMEM((8, 128), f32),
            pltpu.VMEM((16, 8, 128), f32),
            pltpu.VMEM((32, 128), f32),
            pltpu.VMEM((32, 128), f32),
            pltpu.VMEM((16, 64, 1024), f32),
            pltpu.VMEM((1024, 1024), bf16),
            pltpu.VMEM((1024, 1024), bf16),
            pltpu.VMEM((128, 1024), bf16),
            pltpu.VMEM((128, 1024), bf16),
            pltpu.VMEM((128, 1024), bf16),
            dma((4, 2)),
            dma,
            dma((16,)), dma((16,)),
            dma((32,)), dma((32,)),
            dma((16,)), dma((16,)),
            dma((16,)), dma((16,)),
            dma((16,)), dma((16,)),
        ],
        name="influence",
        compiler_params=pltpu.CompilerParams(
            collective_id=0, has_side_effects=True, vmem_limit_bytes=56 << 20
        ),
    )(hidden_acts, out_grads, proj_in.T, proj_out.T, query_codes)


def solution(mesh):
    return jax.shard_map(
        body,
        mesh=mesh,
        in_specs=(
            P("dp", "query"),
            P("dp", "query"),
            P("query", None),
            P("query", None),
            P("query", None),
        ),
        out_specs=P(("dp", "query"), None),
        check_vma=False,
    )
```

```python
import jax
import jax.numpy as jnp
from jax import lax
from jax.experimental import pallas as pl
from jax.experimental.pallas import tpu as pltpu
from jax.sharding import PartitionSpec as P

damping = 0.1
MESH = pl.DeviceIdType.MESH
HIGHEST = lax.Precision.HIGHEST
f32 = jnp.float32
bf16 = jnp.bfloat16


def dot_nt(a, b, precision=None):
    return lax.dot_general(
        a, b, (((1,), (1,)), ((), ())), precision=precision, preferred_element_type=f32
    )


def dot_nn(a, b, precision=None):
    return lax.dot_general(
        a, b, (((1,), (0,)), ((), ())), precision=precision, preferred_element_type=f32
    )


def dot_tn(a, b, precision=None):
    return lax.dot_general(
        a, b, (((0,), (0,)), ((), ())), precision=precision, preferred_element_type=f32
    )


def iota(shape, axis):
    return lax.broadcasted_iota(jnp.int32, shape, axis)


def tile_lanes(x, start):
    lane = iota(x.shape, 1)
    kept = jnp.where((lane >= start) & (lane < start + 32), x, 0.0)
    twice = kept + pltpu.roll(kept, 32, 1)
    return twice + pltpu.roll(twice, 64, 1)


def pack(square):
    lane = iota((8, 128), 1) // 32
    tile = square[0:8]
    for k in range(1, 4):
        tile = jnp.where(lane == k, square[8 * k : 8 * k + 8], tile)
    return tile


def unpack(tile):
    rows = [tile] + [pltpu.roll(tile, 128 - 32 * k, 1) for k in range(1, 4)]
    return jnp.concatenate(rows, axis=0)


def inverse(matrix):
    lane = iota((32, 128), 1)
    row_id = iota((32, 128), 0)
    for k in range(32):
        pivot = 1.0 / matrix[k : k + 1, k : k + 1]
        row = jnp.where(lane[0:1] == k, 1.0, matrix[k : k + 1, :]) * pivot
        column = jnp.where(row_id == k, -1.0, matrix[:, k : k + 1])
        base = jnp.where((lane == k) | (row_id == k), 0.0, matrix)
        matrix = base - column * row
    return matrix


def kernel(
    tokens, hid, grd, wi, wo, codes, out,
    hbuf, gbuf, wip, wop, part, from_left, from_right, eighth, second, third,
    fsend, fpair, ftile, fz, zsum, fp, minv, mpair, q, qhi, qlo, expand, chi, clo,
    weight_sem, load_sem, qload_sem, rs_send, rs_recv, f_send, f_recv,
    qz_send, qz_recv, qp_send, qp_recv, qc_send, qc_recv,
):
    dp = lax.axis_index("dp")
    z = lax.axis_index("query")
    core = lax.rem(dp, 2)
    sibling = dp + 1 - 2 * core

    def at_z(offset):
        return lax.rem(z + offset + 16, 16)

    def chip(i):
        return lax.rem(dp + 2 * i, 32)

    def remote(src, dst, ss, rs, device):
        return pltpu.make_async_remote_copy(
            src_ref=src, dst_ref=dst, send_sem=ss, recv_sem=rs,
            device_id=device, device_id_type=MESH,
        )

    weights_in = []
    for half in range(2):
        for src, dst, at in ((wi, wip, 0), (wo, wop, 32)):
            rows = pl.ds(64 * half + at, 32)
            weights_in.append(pltpu.make_async_copy(
                src, dst.at[half, rows, :], weight_sem.at[len(weights_in)]
            ))
    wip[...] = jnp.zeros_like(wip)
    wop[...] = jnp.zeros_like(wop)
    for copy in weights_in:
        copy.start()
    loads = []
    for g in range(4):
        rows = pl.ds(512 * g, 512)
        loads.append((
            pltpu.make_async_copy(hid.at[rows, :], hbuf.at[rows, :], load_sem.at[g, 0]),
            pltpu.make_async_copy(grd.at[rows, :], gbuf.at[rows, :], load_sem.at[g, 1]),
        ))
        loads[-1][0].start()
        loads[-1][1].start()

    def q_rows(which):
        return pl.ds(pl.multiple_of((which // 8) * 16, 16), 16)

    def q_lanes(which):
        return pl.ds(pl.multiple_of(lax.rem(which, 8) * 128, 128), 128)

    def q_piece(from_z):
        return q.at[from_z, q_rows(dp), q_lanes(dp)]

    def q_block(which):
        return q.at[:, q_rows(which), q_lanes(which)]

    own_q = pltpu.make_async_copy(codes.at[q_rows(dp), q_lanes(dp)], q_piece(z), qload_sem)
    own_q.start()

    barrier = pltpu.get_barrier_semaphore()

    def hello_z(i, carry):
        pl.semaphore_signal(barrier, inc=1, device_id=(dp, at_z(i)), device_id_type=MESH)
        return carry

    def hello_chip(i, carry):
        pl.semaphore_signal(barrier, inc=1, device_id=(chip(i), z), device_id_type=MESH)
        return carry

    lax.fori_loop(1, 16, hello_z, 0)
    lax.fori_loop(1, 16, hello_chip, 0)
    pl.semaphore_signal(barrier, inc=1, device_id=(sibling, z), device_id_type=MESH)

    for copy in weights_in:
        copy.wait()
    for g in range(4):
        loads[g][0].wait()
        loads[g][1].wait()
        total = None
        for half in range(2):
            starts = [512 * g + 128 * j + 64 * half for j in range(4)]
            h = jnp.concatenate([hbuf[s : s + 64, :] for s in starts], axis=0)
            o = jnp.concatenate([gbuf[s : s + 64, :] for s in starts], axis=0)
            term = dot_nt(h, wip[half]) + dot_nt(o, wop[half])
            total = term if total is None else total + term
        part[4 * g : 4 * g + 4] = total.reshape(4, 64, 128)

    expand[...] = jnp.where(
        iota((128, 1024), 1) // 32 == iota((128, 1024), 0), 1.0, 0.0
    ).astype(bf16)

    own_q.wait()
    pl.semaphore_wait(barrier, 31)

    stage1 = []
    for m in (2, -2, 1, -1, 0):
        i = m + 2
        right = remote(part.at[at_z(3 * m + 1)], from_left.at[i],
                       rs_send.at[i], rs_recv.at[i], (dp, at_z(1)))
        left = remote(part.at[at_z(3 * m - 1)], from_right.at[i],
                      rs_send.at[5 + i], rs_recv.at[5 + i], (dp, at_z(-1)))
        right.start()
        left.start()
        stage1 += [right, left]
        if abs(m) == 2:
            s = 0 if m == 2 else 1
            far = remote(part.at[at_z(8), pl.ds(32 * s, 32), :], eighth.at[s],
                         rs_send.at[10 + s], rs_recv.at[10 + s],
                         (dp, at_z(2 if m == 2 else -2)))
            far.start()
            stage1.append(far)
    hub2r, hub2l, far_up, hub_2r, hub_2l, far_down, hub1r, hub1l, hub_1r, hub_1l, hub0r, hub0l = stage1

    spread = []
    for i, offset in enumerate((3, -3, 6, -6, 8)):
        spread.append((remote(q_piece(z), q_piece(z), qz_send.at[i], qz_recv.at[i], (dp, at_z(offset))),
                       remote(q_piece(z), q_piece(at_z(-offset)), qz_send.at[i], qz_recv.at[i], (dp, at_z(offset)))))
        spread[-1][0].start()

    hub2r.wait_recv()
    hub2l.wait_recv()
    far_up.wait_recv()
    part[at_z(6)] = part[at_z(6)] + from_left[4] + from_right[4]
    part[at_z(6), 0:32, :] = part[at_z(6), 0:32, :] + eighth[0]
    up2 = remote(part.at[at_z(6)], second.at[0], rs_send.at[12], rs_recv.at[12], (dp, at_z(3)))
    up2.start()
    hub_2r.wait_recv()
    hub_2l.wait_recv()
    far_down.wait_recv()
    part[at_z(-6)] = part[at_z(-6)] + from_left[0] + from_right[0]
    part[at_z(-6), 32:64, :] = part[at_z(-6), 32:64, :] + eighth[1]
    down2 = remote(part.at[at_z(-6)], second.at[1], rs_send.at[13], rs_recv.at[13], (dp, at_z(-3)))
    down2.start()

    hub1r.wait_recv()
    hub1l.wait_recv()
    hub_1r.wait_recv()
    hub_1l.wait_recv()
    up = part[at_z(3)] + from_left[3] + from_right[3]
    down = part[at_z(-3)] + from_left[1] + from_right[1]
    hub0r.wait_recv()
    hub0l.wait_recv()
    mine = part[z] + from_left[2] + from_right[2]

    for pair in spread:
        pair[1].wait()
    near = []
    for i, offset in enumerate((0, 3, -3, 6, -6)):
        for side, base in ((1, 5), (-1, 10)):
            held, coming = q_piece(at_z(offset)), q_piece(at_z(offset - side))
            sems = (qz_send.at[base + i], qz_recv.at[base + i], (dp, at_z(side)))
            near.append((remote(held, held, *sems), remote(held, coming, *sems)))
            near[-1][0].start()

    up2.wait_recv()
    part[at_z(3)] = up + second[0]
    up3 = remote(part.at[at_z(3)], third.at[0], rs_send.at[14], rs_recv.at[14], (dp, at_z(3)))
    up3.start()
    down2.wait_recv()
    part[at_z(-3)] = down + second[1]
    down3 = remote(part.at[at_z(-3)], third.at[1], rs_send.at[15], rs_recv.at[15], (dp, at_z(-3)))
    down3.start()

    def plane(of_core, a, b):
        x, y = lax.rem(dp // 2, 4), dp // 8
        dx = a * (1 - of_core) + b * of_core
        dy = b * (1 - of_core) + a * of_core
        return (lax.rem(y + dy + 4, 4) * 4 + lax.rem(x + dx + 4, 4)) * 2 + of_core

    def index(a, b):
        return 4 * (a % 4) + b % 4

    q_sent = []

    def q_pass(a, b, da, db):
        i = index(a - da, b - db)
        block = q_block(plane(core, a, b))
        copy = remote(block, block, qp_send.at[i], qp_recv.at[i], (plane(core, da, db), z))
        copy.start()
        q_sent.append(copy)

    def q_split(which):
        for from_z in range(16):
            block = q[from_z, q_rows(which), q_lanes(which)]
            high = block.astype(bf16)
            qhi[from_z, q_rows(which), q_lanes(which)] = high
            qlo[from_z, q_rows(which), q_lanes(which)] = (block - high.astype(f32)).astype(bf16)

    def q_mate(a, b):
        block = q_block(plane(core, a, b))
        i = index(a, b)
        copy = remote(block, block, qc_send.at[i], qc_recv.at[i], (sibling, z))
        copy.start()
        q_sent.append(copy)

    def q_take(a, b):
        i = index(a, b)
        block = q_block(plane(core, a, b))
        remote(block, block, qp_send.at[i], qp_recv.at[i], (sibling, z)).wait_recv()
        q_mate(a, b)

    def q_take_mate(a, b):
        i = index(a, b)
        which = plane(1 - core, a, b)
        remote(q_block(which), q_block(which), qc_send.at[i], qc_recv.at[i], (sibling, z)).wait_recv()
        q_split(which)

    for pair in near:
        pair[1].wait()
    for da, db in ((1, 0), (-1, 0), (0, 1), (0, -1), (2, 0)):
        q_pass(0, 0, da, db)
    q_mate(0, 0)
    q_split(dp)

    up3.wait_recv()
    down3.wait_recv()
    x = mine + third[0] + third[1]

    acts4 = jnp.concatenate([tile_lanes(x, 0), tile_lanes(x, 64)], axis=0)
    grads4 = jnp.concatenate([tile_lanes(x, 32), tile_lanes(x, 96)], axis=0)
    fin = pack(dot_tn(acts4, acts4, HIGHEST)[0:32])
    fout = pack(dot_tn(grads4, grads4, HIGHEST)[0:32])
    first_core = core == 0
    fsend[...] = jnp.where(first_core, fout, fin)
    fisher_pair = remote(fsend, fpair, f_send.at[0], f_recv.at[0], (sibling, z))
    fisher_pair.start()
    keep = jnp.where(first_core, fin, fout)
    fisher_pair.wait_recv()
    ftile[...] = keep + fpair[...]

    def send_fz(i, carry):
        j = lax.rem(i + 7, 15) + 1
        remote(ftile, fz.at[j], f_send.at[j], f_recv.at[j], (dp, at_z(j))).start()
        return carry

    lax.fori_loop(0, 15, send_fz, 0)

    for a in (1, -1):
        q_take(a, 0)
        q_pass(a, 0, 0, 1)
        q_pass(a, 0, 0, -1)
    q_take(0, -1)
    q_pass(0, -1, 0, 1)
    q_take(0, 1)
    q_take(2, 0)
    q_pass(2, 0, 0, 1)
    q_pass(2, 0, 0, -1)
    for a, b in ((1, 0), (-1, 0), (0, 1), (0, -1), (2, 0)):
        q_split(plane(core, a, b))
    q_take_mate(0, 0)

    def wait_fz(i, total):
        remote(ftile, fz.at[i], f_send.at[i], f_recv.at[i], (dp, at_z(i))).wait_recv()
        return total + fz[i]

    zsum[...] = lax.fori_loop(1, 16, wait_fz, ftile[...])

    def send_fp(i, carry):
        remote(zsum, fp.at[i], f_send.at[15 + i], f_recv.at[15 + i], (chip(i), z)).start()
        return carry

    lax.fori_loop(1, 16, send_fp, 0)

    q_take(1, -1)
    q_pass(1, -1, 0, 1)
    q_take(-1, 1)
    q_pass(-1, 1, 0, -1)
    q_take(1, 1)
    q_take(-1, -1)
    for a, b in ((1, -1), (-1, 1), (1, 1), (-1, -1)):
        q_split(plane(core, a, b))
    for a, b in ((1, 0), (-1, 0), (0, 1), (0, -1), (2, 0)):
        q_take_mate(a, b)

    def wait_fp(i, total):
        remote(zsum, fp.at[i], f_send.at[15 + i], f_recv.at[15 + i], (chip(i), z)).wait_recv()
        return total + fp[i]

    fisher = unpack(lax.fori_loop(1, 16, wait_fp, zsum[...]))
    eye = iota((32, 128), 0) == iota((32, 128), 1)
    fisher = fisher / tokens + jnp.where(eye, damping, 0.0)
    minv[...] = inverse(jnp.where(iota((32, 128), 1) < 32, fisher, 0.0))
    swap = remote(minv, mpair, f_send.at[31], f_recv.at[31], (sibling, z))
    swap.start()

    q_take(2, 1)
    q_pass(2, 1, 0, -1)
    q_take(2, -1)
    q_take(0, 2)
    q_take(1, 2)
    q_take(-1, 2)
    for a, b in ((2, 1), (2, -1), (0, 2), (1, 2), (-1, 2)):
        q_split(plane(core, a, b))
    for a, b in ((1, -1), (-1, 1), (1, 1), (-1, -1), (2, 1), (2, -1), (0, 2), (1, 2), (-1, 2)):
        q_take_mate(a, b)
    q_take(2, 2)
    q_split(plane(core, 2, 2))
    q_take_mate(2, 2)

    swap.wait_recv()
    mine_inv, other_inv = minv[...], mpair[...]
    inv_in = tile_lanes(jnp.where(first_core, mine_inv, other_inv), 0)
    inv_out = jnp.where(first_core, other_inv, mine_inv)
    zero = jnp.zeros((32, 128), f32)
    weights = jnp.concatenate([
        jnp.concatenate([inv_in, zero, zero, zero], axis=0),
        jnp.concatenate([zero, zero, inv_in, zero], axis=0),
        jnp.concatenate([zero, inv_out, zero, zero], axis=0),
        jnp.concatenate([zero, zero, zero, inv_out], axis=0),
    ], axis=1)
    ready = dot_nn(x, weights, HIGHEST)
    acts_ready = jnp.concatenate([ready[:, 0:128], ready[:, 128:256]], axis=0)
    grads_ready = jnp.concatenate([ready[:, 256:384], ready[:, 384:512]], axis=0) * (1.0 / 32.0)
    grads_high = grads_ready.astype(bf16)
    grads_low = (grads_ready - grads_high.astype(f32)).astype(bf16)
    for k in range(8):
        lanes = slice(128 * k, 128 * k + 128)
        wide = dot_nn(grads_high, expand[:, lanes]) + dot_nn(grads_low, expand[:, lanes])
        code = wide * acts_ready
        high = code.astype(bf16)
        chi[:, lanes] = high
        clo[:, lanes] = (code - high.astype(f32)).astype(bf16)

    def score(i, carry):
        rows = pl.ds(pl.multiple_of(i * 256, 256), 256)
        four = pl.ds(4 * i, 4)
        high = qhi[four].reshape(256, 1024)
        low = qlo[four].reshape(256, 1024)
        out[:, rows] = dot_nt(chi[...], high) + dot_nt(clo[...], high) + dot_nt(chi[...], low)
        return carry

    lax.fori_loop(0, 4, score, 0)

    for copy in stage1 + [up2, down2, up3, down3, fisher_pair, swap] + q_sent:
        copy.wait_send()

    def sent(i, carry):
        remote(ftile, fz.at[i], f_send.at[i], f_recv.at[i], (dp, at_z(i))).wait_send()
        remote(zsum, fp.at[i], f_send.at[15 + i], f_recv.at[15 + i], (chip(i), z)).wait_send()
        return carry

    lax.fori_loop(1, 16, sent, 0)


def body(hidden_acts, out_grads, proj_in, proj_out, query_codes):
    tokens = float(hidden_acts.shape[0] * lax.axis_size("dp"))
    vmem = pl.BlockSpec(memory_space=pltpu.VMEM)
    hbm = pl.BlockSpec(memory_space=pltpu.HBM)
    dma = pltpu.SemaphoreType.DMA

    def call(*refs):
        kernel(tokens, *refs)

    return pl.pallas_call(
        call,
        out_shape=jax.ShapeDtypeStruct((128, 1024), f32),
        in_specs=[hbm] * 5,
        out_specs=vmem,
        scratch_shapes=[
            pltpu.VMEM((2048, 896), bf16),
            pltpu.VMEM((2048, 256), bf16),
            pltpu.VMEM((2, 128, 896), bf16),
            pltpu.VMEM((2, 128, 256), bf16),
            pltpu.VMEM((16, 64, 128), f32),
            pltpu.VMEM((5, 64, 128), f32),
            pltpu.VMEM((5, 64, 128), f32),
            pltpu.VMEM((2, 32, 128), f32),
            pltpu.VMEM((2, 64, 128), f32),
            pltpu.VMEM((2, 64, 128), f32),
            pltpu.VMEM((8, 128), f32),
            pltpu.VMEM((8, 128), f32),
            pltpu.VMEM((8, 128), f32),
            pltpu.VMEM((16, 8, 128), f32),
            pltpu.VMEM((8, 128), f32),
            pltpu.VMEM((16, 8, 128), f32),
            pltpu.VMEM((32, 128), f32),
            pltpu.VMEM((32, 128), f32),
            pltpu.VMEM((16, 64, 1024), f32),
            pltpu.VMEM((16, 64, 1024), bf16),
            pltpu.VMEM((16, 64, 1024), bf16),
            pltpu.VMEM((128, 1024), bf16),
            pltpu.VMEM((128, 1024), bf16),
            pltpu.VMEM((128, 1024), bf16),
            dma((4,)),
            dma((4, 2)),
            dma,
            dma((16,)), dma((16,)),
            dma((32,)), dma((32,)),
            dma((16,)), dma((16,)),
            dma((16,)), dma((16,)),
            dma((16,)), dma((16,)),
        ],
        name="influence",
        compiler_params=pltpu.CompilerParams(
            collective_id=0, has_side_effects=True, vmem_limit_bytes=56 << 20
        ),
    )(hidden_acts, out_grads, proj_in.T, proj_out.T, query_codes)


def solution(mesh):
    return jax.shard_map(
        body,
        mesh=mesh,
        in_specs=(
            P("dp", "query"),
            P("dp", "query"),
            P("query", None),
            P("query", None),
            P("query", None),
        ),
        out_specs=P(("dp", "query"), None),
        check_vma=False,
    )
```

```python
import jax
import jax.numpy as jnp
from jax import lax
from jax.experimental import pallas as pl
from jax.experimental.pallas import tpu as pltpu
from jax.sharding import PartitionSpec as P

damping = 0.1
MESH = pl.DeviceIdType.MESH
HIGHEST = lax.Precision.HIGHEST
f32 = jnp.float32
bf16 = jnp.bfloat16


def dot_nt(a, b, precision=None):
    return lax.dot_general(
        a, b, (((1,), (1,)), ((), ())), precision=precision, preferred_element_type=f32
    )


def dot_nn(a, b, precision=None):
    return lax.dot_general(
        a, b, (((1,), (0,)), ((), ())), precision=precision, preferred_element_type=f32
    )


def dot_tn(a, b, precision=None):
    return lax.dot_general(
        a, b, (((0,), (0,)), ((), ())), precision=precision, preferred_element_type=f32
    )


def iota(shape, axis):
    return lax.broadcasted_iota(jnp.int32, shape, axis)


def tile_lanes(x, start):
    lane = iota(x.shape, 1)
    kept = jnp.where((lane >= start) & (lane < start + 32), x, 0.0)
    twice = kept + pltpu.roll(kept, 32, 1)
    return twice + pltpu.roll(twice, 64, 1)


def pack(square):
    lane = iota((8, 128), 1) // 32
    tile = square[0:8]
    for k in range(1, 4):
        tile = jnp.where(lane == k, square[8 * k : 8 * k + 8], tile)
    return tile


def unpack(tile):
    rows = [tile] + [pltpu.roll(tile, 128 - 32 * k, 1) for k in range(1, 4)]
    return jnp.concatenate(rows, axis=0)


def inverse(matrix):
    lane = iota((32, 128), 1)
    row_id = iota((32, 128), 0)
    for k in range(0, 32, 2):
        row0, row1 = matrix[k : k + 1, :], matrix[k + 1 : k + 2, :]
        first, cross = matrix[k : k + 1, k : k + 1], matrix[k : k + 1, k + 1 : k + 2]
        last = matrix[k + 1 : k + 2, k + 1 : k + 2]
        inv_first = 1.0 / first
        ratio = cross * inv_first
        inv_last = 1.0 / (last - cross * ratio)
        top, side = inv_first + ratio * ratio * inv_last, -ratio * inv_last
        at0, at1 = lane == k, lane == k + 1
        down0, down1 = row_id == k, row_id == k + 1
        row0 = jnp.where(at0[0:1], 1.0, jnp.where(at1[0:1], 0.0, row0))
        row1 = jnp.where(at1[0:1], 1.0, jnp.where(at0[0:1], 0.0, row1))
        column0 = jnp.where(down0, -1.0, jnp.where(down1, 0.0, matrix[:, k : k + 1]))
        column1 = jnp.where(down1, -1.0, jnp.where(down0, 0.0, matrix[:, k + 1 : k + 2]))
        base = jnp.where(at0 | at1 | down0 | down1, 0.0, matrix)
        new0, new1 = top * row0 + side * row1, side * row0 + inv_last * row1
        matrix = base - column0 * new0 - column1 * new1
    return matrix


def kernel(
    tokens, hid, grd, wi, wo, codes, out,
    hbuf, gbuf, wip, wop, part, from_left, from_right, eighth, second, third,
    fsend, fpair, ftile, fz, zsum, fp, minv, mpair, q, qhi, qlo, expand, chi, clo,
    weight_sem, load_sem, qload_sem, rs_send, rs_recv, f_send, f_recv,
    qz_send, qz_recv, qp_send, qp_recv, qc_send, qc_recv,
):
    dp = lax.axis_index("dp")
    z = lax.axis_index("query")
    core = lax.rem(dp, 2)
    sibling = dp + 1 - 2 * core

    def at_z(offset):
        return lax.rem(z + offset + 16, 16)

    def chip(i):
        return lax.rem(dp + 2 * i, 32)

    def remote(src, dst, ss, rs, device):
        return pltpu.make_async_remote_copy(
            src_ref=src, dst_ref=dst, send_sem=ss, recv_sem=rs,
            device_id=device, device_id_type=MESH,
        )

    weights_in = []
    for half in range(2):
        for src, dst, at in ((wi, wip, 0), (wo, wop, 32)):
            rows = pl.ds(64 * half + at, 32)
            weights_in.append(pltpu.make_async_copy(
                src, dst.at[half, rows, :], weight_sem.at[len(weights_in)]
            ))
    wip[...] = jnp.zeros_like(wip)
    wop[...] = jnp.zeros_like(wop)
    for copy in weights_in:
        copy.start()
    loads = []
    for g in range(4):
        rows = pl.ds(512 * g, 512)
        loads.append((
            pltpu.make_async_copy(hid.at[rows, :], hbuf.at[rows, :], load_sem.at[g, 0]),
            pltpu.make_async_copy(grd.at[rows, :], gbuf.at[rows, :], load_sem.at[g, 1]),
        ))
        loads[-1][0].start()
        loads[-1][1].start()

    def q_rows(which):
        return pl.ds(pl.multiple_of((which // 8) * 16, 16), 16)

    def q_lanes(which):
        return pl.ds(pl.multiple_of(lax.rem(which, 8) * 128, 128), 128)

    def q_piece(from_z):
        return q.at[from_z, q_rows(dp), q_lanes(dp)]

    def q_block(which):
        return q.at[:, q_rows(which), q_lanes(which)]

    own_q = pltpu.make_async_copy(codes.at[q_rows(dp), q_lanes(dp)], q_piece(z), qload_sem)
    own_q.start()

    barrier = pltpu.get_barrier_semaphore()

    def hello_chip(i, carry):
        pl.semaphore_signal(barrier, inc=1, device_id=(chip(i), z), device_id_type=MESH)
        return carry

    for offset in (3, -3, 2, -2, 1, -1):
        pl.semaphore_signal(barrier, inc=1, device_id=(dp, at_z(offset)), device_id_type=MESH)
    lax.fori_loop(1, 16, hello_chip, 0)
    pl.semaphore_signal(barrier, inc=1, device_id=(sibling, z), device_id_type=MESH)

    for copy in weights_in:
        copy.wait()
    for g in range(4):
        loads[g][0].wait()
        loads[g][1].wait()
        total = None
        for half in range(2):
            starts = [512 * g + 128 * j + 64 * half for j in range(4)]
            h = jnp.concatenate([hbuf[s : s + 64, :] for s in starts], axis=0)
            o = jnp.concatenate([gbuf[s : s + 64, :] for s in starts], axis=0)
            term = dot_nt(h, wip[half]) + dot_nt(o, wop[half])
            total = term if total is None else total + term
        part[4 * g : 4 * g + 4] = total.reshape(4, 64, 128)

    expand[...] = jnp.where(
        iota((128, 1024), 1) // 32 == iota((128, 1024), 0), 1.0, 0.0
    ).astype(bf16)

    own_q.wait()
    pl.semaphore_wait(barrier, 22)

    stage1 = []
    for m in (2, -2, 1, -1, 0):
        i = m + 2
        right = remote(part.at[at_z(3 * m + 1)], from_left.at[i],
                       rs_send.at[i], rs_recv.at[i], (dp, at_z(1)))
        left = remote(part.at[at_z(3 * m - 1)], from_right.at[i],
                      rs_send.at[5 + i], rs_recv.at[5 + i], (dp, at_z(-1)))
        right.start()
        left.start()
        stage1 += [right, left]
        if abs(m) == 2:
            s = 0 if m == 2 else 1
            far = remote(part.at[at_z(8), pl.ds(32 * s, 32), :], eighth.at[s],
                         rs_send.at[10 + s], rs_recv.at[10 + s],
                         (dp, at_z(2 if m == 2 else -2)))
            far.start()
            stage1.append(far)
    hub2r, hub2l, far_up, hub_2r, hub_2l, far_down, hub1r, hub1l, hub_1r, hub_1l, hub0r, hub0l = stage1

    def z_pass(i, offset, step):
        held, coming = q_piece(at_z(offset)), q_piece(at_z(offset - step))
        sems = (qz_send.at[i], qz_recv.at[i], (dp, at_z(step)))
        remote(held, held, *sems).start()
        return remote(held, coming, *sems)

    spread = [z_pass(0, 0, 3), z_pass(1, 0, -3)]

    hub2r.wait_recv()
    hub2l.wait_recv()
    far_up.wait_recv()
    part[at_z(6)] = part[at_z(6)] + from_left[4] + from_right[4]
    part[at_z(6), 0:32, :] = part[at_z(6), 0:32, :] + eighth[0]
    up2 = remote(part.at[at_z(6)], second.at[0], rs_send.at[12], rs_recv.at[12], (dp, at_z(3)))
    up2.start()
    hub_2r.wait_recv()
    hub_2l.wait_recv()
    far_down.wait_recv()
    part[at_z(-6)] = part[at_z(-6)] + from_left[0] + from_right[0]
    part[at_z(-6), 32:64, :] = part[at_z(-6), 32:64, :] + eighth[1]
    down2 = remote(part.at[at_z(-6)], second.at[1], rs_send.at[13], rs_recv.at[13], (dp, at_z(-3)))
    down2.start()
    spread[0].wait()
    spread[1].wait()
    spread2 = [z_pass(2, -3, 3), z_pass(3, 3, -3)]

    hub1r.wait_recv()
    hub1l.wait_recv()
    hub_1r.wait_recv()
    hub_1l.wait_recv()
    up = part[at_z(3)] + from_left[3] + from_right[3]
    down = part[at_z(-3)] + from_left[1] + from_right[1]
    hub0r.wait_recv()
    hub0l.wait_recv()
    mine = part[z] + from_left[2] + from_right[2]

    up2.wait_recv()
    part[at_z(3)] = up + second[0]
    up3 = remote(part.at[at_z(3)], third.at[0], rs_send.at[14], rs_recv.at[14], (dp, at_z(3)))
    up3.start()
    down2.wait_recv()
    part[at_z(-3)] = down + second[1]
    down3 = remote(part.at[at_z(-3)], third.at[1], rs_send.at[15], rs_recv.at[15], (dp, at_z(-3)))
    down3.start()
    spread2[0].wait()
    spread2[1].wait()
    near = [z_pass(4, 6, -2)]
    for i, offset in enumerate((0, 3, -3, 6, -6)):
        near += [z_pass(5 + i, offset, 1), z_pass(10 + i, offset, -1)]

    def plane(of_core, a, b):
        x, y = lax.rem(dp // 2, 4), dp // 8
        dx = a * (1 - of_core) + b * of_core
        dy = b * (1 - of_core) + a * of_core
        return (lax.rem(y + dy + 4, 4) * 4 + lax.rem(x + dx + 4, 4)) * 2 + of_core

    def index(a, b):
        return 4 * (a % 4) + b % 4

    q_sent = []

    def q_pass(a, b, da, db):
        i = index(a - da, b - db)
        block = q_block(plane(core, a, b))
        copy = remote(block, block, qp_send.at[i], qp_recv.at[i], (plane(core, da, db), z))
        copy.start()
        q_sent.append(copy)

    def q_split(which):
        for from_z in range(16):
            block = q[from_z, q_rows(which), q_lanes(which)]
            high = block.astype(bf16)
            qhi[from_z, q_rows(which), q_lanes(which)] = high
            qlo[from_z, q_rows(which), q_lanes(which)] = (block - high.astype(f32)).astype(bf16)

    def q_mate(a, b):
        block = q_block(plane(core, a, b))
        i = index(a, b)
        copy = remote(block, block, qc_send.at[i], qc_recv.at[i], (sibling, z))
        copy.start()
        q_sent.append(copy)

    def q_take(a, b):
        i = index(a, b)
        block = q_block(plane(core, a, b))
        remote(block, block, qp_send.at[i], qp_recv.at[i], (sibling, z)).wait_recv()
        q_mate(a, b)

    def q_take_mate(a, b):
        i = index(a, b)
        which = plane(1 - core, a, b)
        remote(q_block(which), q_block(which), qc_send.at[i], qc_recv.at[i], (sibling, z)).wait_recv()
        q_split(which)

    for piece in near:
        piece.wait()
    for da, db in ((1, 0), (-1, 0), (0, 1), (0, -1), (2, 0)):
        q_pass(0, 0, da, db)
    q_mate(0, 0)
    q_split(dp)

    up3.wait_recv()
    down3.wait_recv()
    x = mine + third[0] + third[1]

    acts4 = jnp.concatenate([tile_lanes(x, 0), tile_lanes(x, 64)], axis=0)
    grads4 = jnp.concatenate([tile_lanes(x, 32), tile_lanes(x, 96)], axis=0)
    fin = pack(dot_tn(acts4, acts4, HIGHEST)[0:32])
    fout = pack(dot_tn(grads4, grads4, HIGHEST)[0:32])
    first_core = core == 0
    fsend[...] = jnp.where(first_core, fout, fin)
    fisher_pair = remote(fsend, fpair, f_send.at[0], f_recv.at[0], (sibling, z))
    fisher_pair.start()
    keep = jnp.where(first_core, fin, fout)
    fisher_pair.wait_recv()
    ftile[...] = keep + fpair[...]

    def send_fz(i, carry):
        j = lax.rem(i + 7, 15) + 1
        remote(ftile, fz.at[j], f_send.at[j], f_recv.at[j], (dp, at_z(j))).start()
        return carry

    lax.fori_loop(0, 15, send_fz, 0)

    for a in (1, -1):
        q_take(a, 0)
        q_pass(a, 0, 0, 1)
        q_pass(a, 0, 0, -1)
    q_take(0, -1)
    q_pass(0, -1, 0, 1)
    q_take(0, 1)
    q_take(2, 0)
    q_pass(2, 0, 0, 1)
    q_pass(2, 0, 0, -1)
    for a, b in ((1, 0), (-1, 0), (0, 1), (0, -1), (2, 0)):
        q_split(plane(core, a, b))
    q_take_mate(0, 0)

    def wait_fz(i, total):
        remote(ftile, fz.at[i], f_send.at[i], f_recv.at[i], (dp, at_z(i))).wait_recv()
        return total + fz[i]

    zsum[...] = lax.fori_loop(1, 16, wait_fz, ftile[...])

    def send_fp(i, carry):
        remote(zsum, fp.at[i], f_send.at[15 + i], f_recv.at[15 + i], (chip(i), z)).start()
        return carry

    lax.fori_loop(1, 16, send_fp, 0)

    q_take(1, -1)
    q_pass(1, -1, 0, 1)
    q_take(-1, 1)
    q_pass(-1, 1, 0, -1)
    q_take(2, 1)
    q_pass(2, 1, 0, -1)
    for a, b in ((1, 1), (-1, -1), (0, 2), (2, -1)):
        q_take(a, b)
    for a, b in ((1, -1), (-1, 1), (1, 1), (-1, -1), (2, 1), (0, 2), (2, -1)):
        q_split(plane(core, a, b))
    for a, b in ((1, 0), (-1, 0), (0, 1), (0, -1), (2, 0)):
        q_take_mate(a, b)

    def wait_fp(i, total):
        remote(zsum, fp.at[i], f_send.at[15 + i], f_recv.at[15 + i], (chip(i), z)).wait_recv()
        return total + fp[i]

    fisher = unpack(lax.fori_loop(1, 16, wait_fp, zsum[...]))
    eye = iota((32, 128), 0) == iota((32, 128), 1)
    fisher = fisher / tokens + jnp.where(eye, damping, 0.0)
    minv[...] = inverse(jnp.where(iota((32, 128), 1) < 32, fisher, 0.0))
    swap = remote(minv, mpair, f_send.at[31], f_recv.at[31], (sibling, z))
    swap.start()

    for a, b in ((1, 2), (-1, 2), (2, 2)):
        q_take(a, b)
        q_split(plane(core, a, b))
    for a, b in ((1, -1), (-1, 1), (1, 1), (-1, -1), (2, 1), (0, 2), (2, -1), (1, 2), (-1, 2), (2, 2)):
        q_take_mate(a, b)

    swap.wait_recv()
    mine_inv, other_inv = minv[...], mpair[...]
    inv_in = tile_lanes(jnp.where(first_core, mine_inv, other_inv), 0)
    inv_out = jnp.where(first_core, other_inv, mine_inv)
    zero = jnp.zeros((32, 128), f32)
    weights = jnp.concatenate([
        jnp.concatenate([inv_in, zero, zero, zero], axis=0),
        jnp.concatenate([zero, zero, inv_in, zero], axis=0),
        jnp.concatenate([zero, inv_out, zero, zero], axis=0),
        jnp.concatenate([zero, zero, zero, inv_out], axis=0),
    ], axis=1)
    ready = dot_nn(x, weights, HIGHEST)
    acts_ready = jnp.concatenate([ready[:, 0:128], ready[:, 128:256]], axis=0)
    grads_ready = jnp.concatenate([ready[:, 256:384], ready[:, 384:512]], axis=0) * (1.0 / 32.0)
    grads_high = grads_ready.astype(bf16)
    grads_low = (grads_ready - grads_high.astype(f32)).astype(bf16)
    for k in range(8):
        lanes = slice(128 * k, 128 * k + 128)
        wide = dot_nn(grads_high, expand[:, lanes]) + dot_nn(grads_low, expand[:, lanes])
        code = wide * acts_ready
        high = code.astype(bf16)
        chi[:, lanes] = high
        clo[:, lanes] = (code - high.astype(f32)).astype(bf16)

    def score(i, carry):
        rows = pl.ds(pl.multiple_of(i * 256, 256), 256)
        four = pl.ds(4 * i, 4)
        high = qhi[four].reshape(256, 1024)
        low = qlo[four].reshape(256, 1024)
        out[:, rows] = dot_nt(chi[...], high) + dot_nt(clo[...], high) + dot_nt(chi[...], low)
        return carry

    lax.fori_loop(0, 4, score, 0)

    for copy in stage1 + [up2, down2, up3, down3, fisher_pair, swap] + q_sent:
        copy.wait_send()

    def sent(i, carry):
        remote(ftile, fz.at[i], f_send.at[i], f_recv.at[i], (dp, at_z(i))).wait_send()
        remote(zsum, fp.at[i], f_send.at[15 + i], f_recv.at[15 + i], (chip(i), z)).wait_send()
        return carry

    lax.fori_loop(1, 16, sent, 0)


def body(hidden_acts, out_grads, proj_in, proj_out, query_codes):
    tokens = float(hidden_acts.shape[0] * lax.axis_size("dp"))
    vmem = pl.BlockSpec(memory_space=pltpu.VMEM)
    hbm = pl.BlockSpec(memory_space=pltpu.HBM)
    dma = pltpu.SemaphoreType.DMA

    def call(*refs):
        kernel(tokens, *refs)

    return pl.pallas_call(
        call,
        out_shape=pltpu.VMEM((128, 1024), f32),
        in_specs=[hbm] * 5,
        out_specs=vmem,
        scratch_shapes=[
            pltpu.VMEM((2048, 896), bf16),
            pltpu.VMEM((2048, 256), bf16),
            pltpu.VMEM((2, 128, 896), bf16),
            pltpu.VMEM((2, 128, 256), bf16),
            pltpu.VMEM((16, 64, 128), f32),
            pltpu.VMEM((5, 64, 128), f32),
            pltpu.VMEM((5, 64, 128), f32),
            pltpu.VMEM((2, 32, 128), f32),
            pltpu.VMEM((2, 64, 128), f32),
            pltpu.VMEM((2, 64, 128), f32),
            pltpu.VMEM((8, 128), f32),
            pltpu.VMEM((8, 128), f32),
            pltpu.VMEM((8, 128), f32),
            pltpu.VMEM((16, 8, 128), f32),
            pltpu.VMEM((8, 128), f32),
            pltpu.VMEM((16, 8, 128), f32),
            pltpu.VMEM((32, 128), f32),
            pltpu.VMEM((32, 128), f32),
            pltpu.VMEM((16, 64, 1024), f32),
            pltpu.VMEM((16, 64, 1024), bf16),
            pltpu.VMEM((16, 64, 1024), bf16),
            pltpu.VMEM((128, 1024), bf16),
            pltpu.VMEM((128, 1024), bf16),
            pltpu.VMEM((128, 1024), bf16),
            dma((4,)),
            dma((4, 2)),
            dma,
            dma((16,)), dma((16,)),
            dma((32,)), dma((32,)),
            dma((16,)), dma((16,)),
            dma((16,)), dma((16,)),
            dma((16,)), dma((16,)),
        ],
        name="influence",
        compiler_params=pltpu.CompilerParams(
            collective_id=0, has_side_effects=True, vmem_limit_bytes=24 << 20
        ),
    )(*[
        pltpu.with_memory_space_constraint(a, pltpu.HBM)
        for a in (hidden_acts, out_grads, proj_in.T, proj_out.T, query_codes)
    ])


def solution(mesh):
    return jax.shard_map(
        body,
        mesh=mesh,
        in_specs=(
            P("dp", "query"),
            P("dp", "query"),
            P("query", None),
            P("query", None),
            P("query", None),
        ),
        out_specs=P(("dp", "query"), None),
        check_vma=False,
    )
```

```python
import jax
import jax.numpy as jnp
from jax import lax
from jax.experimental import pallas as pl
from jax.experimental.pallas import tpu as pltpu
from jax.sharding import PartitionSpec as P

damping = 0.1
MESH = pl.DeviceIdType.MESH
HIGHEST = lax.Precision.HIGHEST
f32 = jnp.float32
bf16 = jnp.bfloat16


def dot_nt(a, b, precision=None):
    return lax.dot_general(
        a, b, (((1,), (1,)), ((), ())), precision=precision, preferred_element_type=f32
    )


def dot_nn(a, b, precision=None):
    return lax.dot_general(
        a, b, (((1,), (0,)), ((), ())), precision=precision, preferred_element_type=f32
    )


def dot_tn(a, b, precision=None):
    return lax.dot_general(
        a, b, (((0,), (0,)), ((), ())), precision=precision, preferred_element_type=f32
    )


def iota(shape, axis):
    return lax.broadcasted_iota(jnp.int32, shape, axis)


def tile_lanes(x, start):
    lane = iota(x.shape, 1)
    kept = jnp.where((lane >= start) & (lane < start + 32), x, 0.0)
    twice = kept + pltpu.roll(kept, 32, 1)
    return twice + pltpu.roll(twice, 64, 1)


def factors(product):
    lane = iota((32, 128), 1) // 32

    def block(k):
        kept = jnp.where(lane == k, product[32 * k : 32 * k + 32], 0.0)
        return pltpu.roll(kept, 128 - 32 * k, 1) if k else kept

    def pack(square):
        tile = square[0:8]
        for k in range(1, 4):
            tile = tile + pltpu.roll(square[8 * k : 8 * k + 8], 32 * k, 1)
        return tile

    return pack(block(0) + block(2)), pack(block(1) + block(3))


def unpack(tile):
    rows = [tile] + [pltpu.roll(tile, 128 - 32 * k, 1) for k in range(1, 4)]
    return jnp.concatenate(rows, axis=0)


def inverse(matrix):
    lane = iota((1, 128), 1)
    row_id = iota((8, 128), 0)
    tiles = [matrix[8 * t : 8 * t + 8] for t in range(4)]
    for b in range(4):
        spread = [
            [jnp.broadcast_to(tiles[t][:, 8 * b + j : 8 * b + j + 1], (8, 128)) for t in range(4)]
            for j in range(8)
        ]
        for j in range(8):
            k = 8 * b + j
            columns = spread[j]
            pivot = 1.0 / columns[b][j : j + 1]
            row = jnp.where(lane == k, 1.0, tiles[b][j : j + 1]) * pivot
            factors_next = [columns[b][n : n + 1] * pivot for n in range(j + 1, 8)]
            columns = [jnp.where(row_id == j, -1.0, c) if t == b else c for t, c in enumerate(columns)]
            for t in range(4):
                kept = jnp.where(lane == k, 0.0, tiles[t])
                if t == b:
                    kept = jnp.where(row_id == j, 0.0, kept)
                tiles[t] = kept - columns[t] * row
            for n, factor in zip(range(j + 1, 8), factors_next):
                for t in range(4):
                    kept = spread[n][t]
                    if t == b:
                        kept = jnp.where(row_id == j, 0.0, kept)
                    spread[n][t] = kept - columns[t] * factor
    return jnp.concatenate(tiles, axis=0)


def kernel(
    tokens, hid, grd, wi, wo, codes, out,
    hbuf, gbuf, proj, part, from_left, from_right, eighth, second, third,
    fsend, fpair, ftile, fz, zsum, fp, minv, mpair, q, qhi, qlo, expand, code_parts,
    weight_sem, load_sem, qload_sem, rs_send, rs_recv, f_send, f_recv,
    qz_send, qz_recv, qp_send, qp_recv, qc_send, qc_recv,
):
    dp = lax.axis_index("dp")
    z = lax.axis_index("query")
    core = lax.rem(dp, 2)
    sibling = dp + 1 - 2 * core

    def at_z(offset):
        return lax.rem(z + offset + 16, 16)

    def chip(i):
        return lax.rem(dp + 2 * i, 32)

    def rel(offset):
        return (offset - 5) % 16

    def remote(src, dst, ss, rs, device):
        return pltpu.make_async_remote_copy(
            src_ref=src, dst_ref=dst, send_sem=ss, recv_sem=rs,
            device_id=device, device_id_type=MESH,
        )

    barrier = pltpu.get_barrier_semaphore()

    def hello_chip(i, carry):
        pl.semaphore_signal(barrier, inc=1, device_id=(chip(i), z), device_id_type=MESH)
        return carry

    for offset in (3, -3, 2, -2, 1, -1):
        pl.semaphore_signal(barrier, inc=1, device_id=(dp, at_z(offset)), device_id_type=MESH)
    lax.fori_loop(1, 16, hello_chip, 0)
    pl.semaphore_signal(barrier, inc=1, device_id=(sibling, z), device_id_type=MESH)

    weights_in = []
    for half in range(2):
        for src, start, width, at in ((wi, 0, 896, 0), (wo, 896, 256, 32)):
            rows = pl.ds(64 * half + at, 32)
            lanes = pl.ds(1152 * half + start, width)
            weights_in.append(pltpu.make_async_copy(
                src, proj.at[rows, lanes], weight_sem.at[len(weights_in)]
            ))
    proj[...] = jnp.zeros_like(proj)
    for copy in weights_in:
        copy.start()
    loads = []
    chunks = ((0, 7), (7, 9))
    for g, (start, count) in enumerate(chunks):
        def load(j, carry, g=g):
            rows = pl.ds(pl.multiple_of(at_z(5 + j) * 128, 128), 128)
            pltpu.make_async_copy(hid.at[rows, :], hbuf.at[j], load_sem.at[g, 0]).start()
            pltpu.make_async_copy(grd.at[rows, :], gbuf.at[j], load_sem.at[g, 1]).start()
            return carry

        lax.fori_loop(start, start + count, load, 0)
        held = pl.ds(start, count)
        loads.append((
            pltpu.make_async_copy(hbuf.at[held], hbuf.at[held], load_sem.at[g, 0]),
            pltpu.make_async_copy(gbuf.at[held], gbuf.at[held], load_sem.at[g, 1]),
        ))

    def q_rows(which):
        return pl.ds(pl.multiple_of((which // 8) * 16, 16), 16)

    def q_lanes(which):
        return pl.ds(pl.multiple_of(lax.rem(which, 8) * 128, 128), 128)

    def q_piece(from_z):
        return q.at[from_z, q_rows(dp), q_lanes(dp)]

    def q_block(which):
        return q.at[:, q_rows(which), q_lanes(which)]

    own_q = pltpu.make_async_copy(codes.at[q_rows(dp), q_lanes(dp)], q_piece(z), qload_sem)
    own_q.start()

    for copy in weights_in:
        copy.wait()

    def project(g):
        start, count = chunks[g]
        loads[g][0].wait()
        loads[g][1].wait()
        total = None
        for half in range(2):
            rows = slice(64 * half, 64 * half + 64)
            for ref, lane, width in ((hbuf, 0, 896), (gbuf, 896, 256)):
                left = ref[start : start + count, rows, :].reshape(64 * count, width)
                lane = lane + 1152 * half
                term = dot_nt(left, proj[:, lane : lane + width])
                total = term if total is None else total + term
        part[start : start + count] = total.reshape(count, 64, 128)

    stage1 = []

    def to_hub(m):
        i = m + 2
        right = remote(part.at[rel(3 * m + 1)], from_left.at[i],
                       rs_send.at[i], rs_recv.at[i], (dp, at_z(1)))
        left = remote(part.at[rel(3 * m - 1)], from_right.at[i],
                      rs_send.at[5 + i], rs_recv.at[5 + i], (dp, at_z(-1)))
        right.start()
        left.start()
        stage1.extend([right, left])
        if abs(m) == 2:
            s = 0 if m == 2 else 1
            far = remote(part.at[rel(8), pl.ds(32 * s, 32), :], eighth.at[s],
                         rs_send.at[10 + s], rs_recv.at[10 + s], (dp, at_z(m)))
            far.start()
            stage1.append(far)

    def z_pass(i, offset, step):
        held, coming = q_piece(at_z(offset)), q_piece(at_z(offset - step))
        sems = (qz_send.at[i], qz_recv.at[i], (dp, at_z(step)))
        remote(held, held, *sems).start()
        return remote(held, coming, *sems)

    project(0)
    own_q.wait()
    pl.semaphore_wait(barrier, 22)
    to_hub(2)
    to_hub(-2)
    spread = [z_pass(0, 0, 3), z_pass(1, 0, -3)]
    project(1)
    to_hub(1)
    to_hub(-1)
    to_hub(0)
    hub2r, hub2l, far_up, hub_2r, hub_2l, far_down, hub1r, hub1l, hub_1r, hub_1l, hub0r, hub0l = stage1

    spread[0].wait()
    spread[1].wait()
    spread2 = [z_pass(2, -3, 3), z_pass(3, 3, -3)]

    halves = (slice(0, 32), slice(32, 64))

    def half_pass(i, src, dst, half, step):
        copy = remote(src.at[pl.ds(32 * half, 32), :], dst.at[pl.ds(32 * half, 32), :],
                      rs_send.at[i], rs_recv.at[i], (dp, at_z(step)))
        copy.start()
        return copy

    hub2r.wait_recv()
    hub2l.wait_recv()
    far_up.wait_recv()
    part[rel(6)] = part[rel(6)] + from_left[4] + from_right[4]
    part[rel(6), 0:32, :] = part[rel(6), 0:32, :] + eighth[0]
    up2 = [half_pass(12, part.at[rel(6)], second.at[0], 0, 3)]
    hub_2r.wait_recv()
    hub_2l.wait_recv()
    far_down.wait_recv()
    part[rel(-6)] = part[rel(-6)] + from_left[0] + from_right[0]
    part[rel(-6), 32:64, :] = part[rel(-6), 32:64, :] + eighth[1]
    down2 = [half_pass(13, part.at[rel(-6)], second.at[1], 0, -3)]
    up2.append(half_pass(14, part.at[rel(6)], second.at[0], 1, 3))
    down2.append(half_pass(15, part.at[rel(-6)], second.at[1], 1, -3))

    hub1r.wait_recv()
    hub1l.wait_recv()
    hub_1r.wait_recv()
    hub_1l.wait_recv()
    up = part[rel(3)] + from_left[3] + from_right[3]
    down = part[rel(-3)] + from_left[1] + from_right[1]
    hub0r.wait_recv()
    hub0l.wait_recv()
    mine = part[rel(0)] + from_left[2] + from_right[2]

    expand[...] = jnp.where(
        iota((128, 1024), 1) // 32 == iota((128, 1024), 0), 1.0, 0.0
    ).astype(bf16)

    spread2[0].wait()
    spread2[1].wait()
    near = [z_pass(4, 6, -2)]
    for i, offset in enumerate((0, 3, -3, 6, -6)):
        near += [z_pass(5 + i, offset, 1), z_pass(10 + i, offset, -1)]

    up3, down3 = [], []
    for h, rows in enumerate(halves):
        up2[h].wait_recv()
        part[rel(3), rows, :] = up[rows] + second[0, rows, :]
        up3.append(half_pass(16 + h, part.at[rel(3)], third.at[0], h, 3))
        down2[h].wait_recv()
        part[rel(-3), rows, :] = down[rows] + second[1, rows, :]
        down3.append(half_pass(18 + h, part.at[rel(-3)], third.at[1], h, -3))

    def plane(of_core, a, b):
        x, y = lax.rem(dp // 2, 4), dp // 8
        dx = a * (1 - of_core) + b * of_core
        dy = b * (1 - of_core) + a * of_core
        return (lax.rem(y + dy + 4, 4) * 4 + lax.rem(x + dx + 4, 4)) * 2 + of_core

    def index(a, b):
        return 4 * (a % 4) + b % 4

    q_sent = []

    def q_pass(a, b, da, db):
        i = index(a - da, b - db)
        block = q_block(plane(core, a, b))
        copy = remote(block, block, qp_send.at[i], qp_recv.at[i], (plane(core, da, db), z))
        copy.start()
        q_sent.append(copy)

    def q_split(which):
        for from_z in range(16):
            block = q[from_z, q_rows(which), q_lanes(which)]
            high = block.astype(bf16)
            qhi[from_z, q_rows(which), q_lanes(which)] = high
            qlo[from_z, q_rows(which), q_lanes(which)] = (block - high.astype(f32)).astype(bf16)

    def q_mate(a, b):
        block = q_block(plane(core, a, b))
        i = index(a, b)
        copy = remote(block, block, qc_send.at[i], qc_recv.at[i], (sibling, z))
        copy.start()
        q_sent.append(copy)

    def q_take(a, b):
        i = index(a, b)
        block = q_block(plane(core, a, b))
        remote(block, block, qp_send.at[i], qp_recv.at[i], (sibling, z)).wait_recv()
        q_mate(a, b)

    def q_take_mate(a, b):
        i = index(a, b)
        which = plane(1 - core, a, b)
        remote(q_block(which), q_block(which), qc_send.at[i], qc_recv.at[i], (sibling, z)).wait_recv()
        q_split(which)

    for piece in near:
        piece.wait()
    for da, db in ((1, 0), (-1, 0), (0, 1), (0, -1), (2, 0)):
        q_pass(0, 0, da, db)
    q_mate(0, 0)
    q_split(dp)

    for copy in up3 + down3:
        copy.wait_recv()
    x = mine + third[0] + third[1]

    fin, fout = factors(dot_tn(x, x, HIGHEST))
    first_core = core == 0
    fsend[...] = jnp.where(first_core, fout, fin)
    fisher_pair = remote(fsend, fpair, f_send.at[0], f_recv.at[0], (sibling, z))
    fisher_pair.start()
    keep = jnp.where(first_core, fin, fout)
    fisher_pair.wait_recv()
    ftile[...] = keep + fpair[...]

    def send_fz(i, carry):
        j = lax.rem(i + 7, 15) + 1
        remote(ftile, fz.at[j], f_send.at[j], f_recv.at[j], (dp, at_z(j))).start()
        return carry

    lax.fori_loop(0, 15, send_fz, 0)

    for a in (1, -1):
        q_take(a, 0)
        q_pass(a, 0, 0, 1)
        q_pass(a, 0, 0, -1)
    q_take(0, -1)
    q_pass(0, -1, 0, 1)
    q_take(0, 1)
    q_take(2, 0)
    q_pass(2, 0, 0, 1)
    q_pass(2, 0, 0, -1)
    for a, b in ((1, 0), (-1, 0), (0, 1), (0, -1), (2, 0)):
        q_split(plane(core, a, b))
    q_take_mate(0, 0)

    def wait_fz(i, total):
        remote(ftile, fz.at[i], f_send.at[i], f_recv.at[i], (dp, at_z(i))).wait_recv()
        return total + fz[i]

    zsum[...] = lax.fori_loop(1, 16, wait_fz, ftile[...])

    def send_fp(i, carry):
        remote(zsum, fp.at[i], f_send.at[15 + i], f_recv.at[15 + i], (chip(i), z)).start()
        return carry

    lax.fori_loop(1, 16, send_fp, 0)

    q_take(1, -1)
    q_pass(1, -1, 0, 1)
    q_take(-1, 1)
    q_pass(-1, 1, 0, -1)
    q_take(2, 1)
    q_pass(2, 1, 0, -1)
    for a, b in ((1, 1), (-1, -1), (0, 2), (2, -1)):
        q_take(a, b)
    for a, b in ((1, -1), (-1, 1), (1, 1), (-1, -1), (2, 1), (0, 2), (2, -1)):
        q_split(plane(core, a, b))
    for a, b in ((1, 0), (-1, 0), (0, 1), (0, -1), (2, 0)):
        q_take_mate(a, b)

    def wait_fp(i, total):
        remote(zsum, fp.at[i], f_send.at[15 + i], f_recv.at[15 + i], (chip(i), z)).wait_recv()
        return total + fp[i]

    fisher = unpack(lax.fori_loop(1, 16, wait_fp, zsum[...]))
    eye = iota((32, 128), 0) == iota((32, 128), 1)
    fisher = fisher / tokens + jnp.where(eye, damping, 0.0)
    minv[...] = inverse(jnp.where(iota((32, 128), 1) < 32, fisher, 0.0))
    swap = remote(minv, mpair, f_send.at[31], f_recv.at[31], (sibling, z))
    swap.start()

    for a, b in ((1, 2), (-1, 2), (2, 2)):
        q_take(a, b)
        q_split(plane(core, a, b))
    for a, b in ((1, -1), (-1, 1), (1, 1), (-1, -1), (2, 1), (0, 2), (2, -1), (1, 2), (-1, 2), (2, 2)):
        q_take_mate(a, b)

    swap.wait_recv()
    mine_inv, other_inv = minv[...], mpair[...]
    inv_in = tile_lanes(jnp.where(first_core, mine_inv, other_inv), 0)
    inv_out = jnp.where(first_core, other_inv, mine_inv)
    zero = jnp.zeros((32, 128), f32)
    weights = jnp.concatenate([
        jnp.concatenate([inv_in, zero, zero, zero], axis=0),
        jnp.concatenate([zero, zero, inv_in, zero], axis=0),
        jnp.concatenate([zero, inv_out, zero, zero], axis=0),
        jnp.concatenate([zero, zero, zero, inv_out], axis=0),
    ], axis=1)
    ready = dot_nn(x, weights, HIGHEST)
    acts_ready = jnp.concatenate([ready[:, 0:128], ready[:, 128:256]], axis=0)
    grads_ready = jnp.concatenate([ready[:, 256:384], ready[:, 384:512]], axis=0) * (1.0 / 32.0)
    grads_high = grads_ready.astype(bf16)
    grads_low = (grads_ready - grads_high.astype(f32)).astype(bf16)
    for k in range(8):
        lanes = slice(128 * k, 128 * k + 128)
        wide = dot_nn(grads_high, expand[:, lanes]) + dot_nn(grads_low, expand[:, lanes])
        code = wide * acts_ready
        high = code.astype(bf16)
        code_parts[0:128, lanes] = high
        code_parts[128:256, lanes] = (code - high.astype(f32)).astype(bf16)

    def score(i, carry):
        rows = pl.ds(pl.multiple_of(i * 256, 256), 256)
        four = pl.ds(4 * i, 4)
        high = qhi[four].reshape(256, 1024)
        low = qlo[four].reshape(256, 1024)
        by_high = dot_nt(code_parts[...], high)
        out[:, rows] = by_high[0:128] + by_high[128:256] + dot_nt(code_parts[0:128, :], low)
        return carry

    lax.fori_loop(0, 4, score, 0)

    for copy in stage1 + up2 + down2 + up3 + down3 + [fisher_pair, swap] + q_sent:
        copy.wait_send()

    def sent(i, carry):
        remote(ftile, fz.at[i], f_send.at[i], f_recv.at[i], (dp, at_z(i))).wait_send()
        remote(zsum, fp.at[i], f_send.at[15 + i], f_recv.at[15 + i], (chip(i), z)).wait_send()
        return carry

    lax.fori_loop(1, 16, sent, 0)


def body(hidden_acts, out_grads, proj_in, proj_out, query_codes):
    tokens = float(hidden_acts.shape[0] * lax.axis_size("dp"))
    vmem = pl.BlockSpec(memory_space=pltpu.VMEM)
    hbm = pl.BlockSpec(memory_space=pltpu.HBM)
    dma = pltpu.SemaphoreType.DMA

    def call(*refs):
        kernel(tokens, *refs)

    return pl.pallas_call(
        call,
        out_shape=pltpu.VMEM((128, 1024), f32),
        in_specs=[hbm] * 5,
        out_specs=vmem,
        scratch_shapes=[
            pltpu.VMEM((16, 128, 896), bf16),
            pltpu.VMEM((16, 128, 256), bf16),
            pltpu.VMEM((128, 2304), bf16),
            pltpu.VMEM((16, 64, 128), f32),
            pltpu.VMEM((5, 64, 128), f32),
            pltpu.VMEM((5, 64, 128), f32),
            pltpu.VMEM((2, 32, 128), f32),
            pltpu.VMEM((2, 64, 128), f32),
            pltpu.VMEM((2, 64, 128), f32),
            pltpu.VMEM((8, 128), f32),
            pltpu.VMEM((8, 128), f32),
            pltpu.VMEM((8, 128), f32),
            pltpu.VMEM((16, 8, 128), f32),
            pltpu.VMEM((8, 128), f32),
            pltpu.VMEM((16, 8, 128), f32),
            pltpu.VMEM((32, 128), f32),
            pltpu.VMEM((32, 128), f32),
            pltpu.VMEM((16, 64, 1024), f32),
            pltpu.VMEM((16, 64, 1024), bf16),
            pltpu.VMEM((16, 64, 1024), bf16),
            pltpu.VMEM((128, 1024), bf16),
            pltpu.VMEM((256, 1024), bf16),
            dma((4,)),
            dma((2, 2)),
            dma,
            dma((20,)), dma((20,)),
            dma((32,)), dma((32,)),
            dma((16,)), dma((16,)),
            dma((16,)), dma((16,)),
            dma((16,)), dma((16,)),
        ],
        name="influence",
        compiler_params=pltpu.CompilerParams(
            collective_id=0, has_side_effects=True, vmem_limit_bytes=24 << 20
        ),
    )(*[
        pltpu.with_memory_space_constraint(a, pltpu.HBM)
        for a in (hidden_acts, out_grads, proj_in.T, proj_out.T, query_codes)
    ])


def solution(mesh):
    return jax.shard_map(
        body,
        mesh=mesh,
        in_specs=(
            P("dp", "query"),
            P("dp", "query"),
            P("query", None),
            P("query", None),
            P("query", None),
        ),
        out_specs=P(("dp", "query"), None),
        check_vma=False,
    )
```

```python
import jax
import jax.numpy as jnp
from jax import lax
from jax.experimental import pallas as pl
from jax.experimental.pallas import tpu as pltpu
from jax.sharding import PartitionSpec as P

damping = 0.1
MESH = pl.DeviceIdType.MESH
HIGHEST = lax.Precision.HIGHEST
f32 = jnp.float32
bf16 = jnp.bfloat16


def dot_nt(a, b, precision=None):
    return lax.dot_general(
        a, b, (((1,), (1,)), ((), ())), precision=precision, preferred_element_type=f32
    )


def dot_nn(a, b, precision=None):
    return lax.dot_general(
        a, b, (((1,), (0,)), ((), ())), precision=precision, preferred_element_type=f32
    )


def dot_tn(a, b, precision=None):
    return lax.dot_general(
        a, b, (((0,), (0,)), ((), ())), precision=precision, preferred_element_type=f32
    )


def iota(shape, axis):
    return lax.broadcasted_iota(jnp.int32, shape, axis)


def factors(product):
    lane = iota((32, 128), 1) // 32

    def block(k):
        kept = jnp.where(lane == k, product[32 * k : 32 * k + 32], 0.0)
        return pltpu.roll(kept, 128 - 32 * k, 1) if k else kept

    def pack(square):
        tile = square[0:8]
        for k in range(1, 4):
            tile = tile + pltpu.roll(square[8 * k : 8 * k + 8], 32 * k, 1)
        return tile

    return pack(block(0) + block(2)), pack(block(1) + block(3))


def unpack(tile):
    rows = [tile] + [pltpu.roll(tile, 128 - 32 * k, 1) for k in range(1, 4)]
    return jnp.concatenate(rows, axis=0)


def inverse(matrix):
    lane = iota((1, 128), 1)
    row_id = iota((8, 128), 0)
    tiles = [matrix[8 * t : 8 * t + 8] for t in range(4)]
    for b in range(4):
        spread = [
            [jnp.broadcast_to(tiles[t][:, 8 * b + j : 8 * b + j + 1], (8, 128)) for t in range(4)]
            for j in range(8)
        ]
        for j in range(8):
            k = 8 * b + j
            columns = spread[j]
            pivot = 1.0 / columns[b][j : j + 1]
            row = jnp.where(lane == k, 1.0, tiles[b][j : j + 1]) * pivot
            factors_next = [columns[b][n : n + 1] * pivot for n in range(j + 1, 8)]
            columns = [jnp.where(row_id == j, -1.0, c) if t == b else c for t, c in enumerate(columns)]
            for t in range(4):
                kept = jnp.where(lane == k, 0.0, tiles[t])
                if t == b:
                    kept = jnp.where(row_id == j, 0.0, kept)
                tiles[t] = kept - columns[t] * row
            for n, factor in zip(range(j + 1, 8), factors_next):
                for t in range(4):
                    kept = spread[n][t]
                    if t == b:
                        kept = jnp.where(row_id == j, 0.0, kept)
                    spread[n][t] = kept - columns[t] * factor
    return jnp.concatenate(tiles, axis=0)


def kernel(
    tokens, hid, grd, wi, wo, codes, out,
    hbuf, gbuf, proj, part, from_left, from_right, eighth, second, third,
    fsend, fpair, ftile, fz, zsum, fp, minv, mpair, q, qhi, qlo, code_parts,
    weight_sem, load_sem, qload_sem, rs_send, rs_recv, f_send, f_recv, fsum_send, fsum_recv,
    qz_send, qz_recv, qp_send, qp_recv, qc_send, qc_recv,
):
    dp = lax.axis_index("dp")
    z = lax.axis_index("query")
    core = lax.rem(dp, 2)
    sibling = dp + 1 - 2 * core

    def at_z(offset):
        return lax.rem(z + offset + 16, 16)

    def chip(i):
        return lax.rem(dp + 2 * i, 32)

    def rel(offset):
        return (offset - 5) % 16

    def remote(src, dst, ss, rs, device):
        return pltpu.make_async_remote_copy(
            src_ref=src, dst_ref=dst, send_sem=ss, recv_sem=rs,
            device_id=device, device_id_type=MESH,
        )

    barrier = pltpu.get_barrier_semaphore()

    def hello_chip(i, carry):
        pl.semaphore_signal(barrier, inc=1, device_id=(chip(i), z), device_id_type=MESH)
        return carry

    for offset in (3, -3, 2, -2, 1, -1):
        pl.semaphore_signal(barrier, inc=1, device_id=(dp, at_z(offset)), device_id_type=MESH)
    lax.fori_loop(1, 16, hello_chip, 0)
    pl.semaphore_signal(barrier, inc=1, device_id=(sibling, z), device_id_type=MESH)

    weights_in = []
    for half in range(2):
        for src, start, width, at in ((wi, 0, 896, 0), (wo, 896, 256, 32)):
            rows = pl.ds(64 * half + at, 32)
            lanes = pl.ds(1152 * half + start, width)
            weights_in.append(pltpu.make_async_copy(
                src, proj.at[rows, lanes], weight_sem.at[len(weights_in)]
            ))
    proj[...] = jnp.zeros_like(proj)
    for copy in weights_in:
        copy.start()
    loads = []
    chunks = ((0, 7), (7, 9))
    for g, (start, count) in enumerate(chunks):
        def load(j, carry, g=g):
            rows = pl.ds(pl.multiple_of(at_z(5 + j) * 128, 128), 128)
            pltpu.make_async_copy(hid.at[rows, :], hbuf.at[j], load_sem.at[g, 0]).start()
            pltpu.make_async_copy(grd.at[rows, :], gbuf.at[j], load_sem.at[g, 1]).start()
            return carry

        lax.fori_loop(start, start + count, load, 0)
        held = pl.ds(start, count)
        loads.append((
            pltpu.make_async_copy(hbuf.at[held], hbuf.at[held], load_sem.at[g, 0]),
            pltpu.make_async_copy(gbuf.at[held], gbuf.at[held], load_sem.at[g, 1]),
        ))

    def q_rows(which):
        return pl.ds(pl.multiple_of((which // 8) * 16, 16), 16)

    def q_lanes(which):
        return pl.ds(pl.multiple_of(lax.rem(which, 8) * 128, 128), 128)

    def q_piece(from_z):
        return q.at[from_z, q_rows(dp), q_lanes(dp)]

    def q_block(which):
        return q.at[:, q_rows(which), q_lanes(which)]

    own_q = pltpu.make_async_copy(codes.at[q_rows(dp), q_lanes(dp)], q_piece(z), qload_sem)
    own_q.start()

    for copy in weights_in:
        copy.wait()

    def project(g):
        start, count = chunks[g]
        loads[g][0].wait()
        loads[g][1].wait()
        total = None
        for half in range(2):
            rows = slice(64 * half, 64 * half + 64)
            for ref, lane, width in ((hbuf, 0, 896), (gbuf, 896, 256)):
                left = ref[start : start + count, rows, :].reshape(64 * count, width)
                lane = lane + 1152 * half
                term = dot_nt(left, proj[:, lane : lane + width])
                total = term if total is None else total + term
        part[start : start + count] = total.reshape(count, 64, 128)

    stage1 = []

    def to_hub(m):
        i = m + 2
        right = remote(part.at[rel(3 * m + 1)], from_left.at[i],
                       rs_send.at[i], rs_recv.at[i], (dp, at_z(1)))
        left = remote(part.at[rel(3 * m - 1)], from_right.at[i],
                      rs_send.at[5 + i], rs_recv.at[5 + i], (dp, at_z(-1)))
        right.start()
        left.start()
        stage1.extend([right, left])
        if abs(m) == 2:
            s = 0 if m == 2 else 1
            far = remote(part.at[rel(8), pl.ds(32 * s, 32), :], eighth.at[s],
                         rs_send.at[10 + s], rs_recv.at[10 + s], (dp, at_z(m)))
            far.start()
            stage1.append(far)

    def z_pass(i, offset, step):
        held, coming = q_piece(at_z(offset)), q_piece(at_z(offset - step))
        sems = (qz_send.at[i], qz_recv.at[i], (dp, at_z(step)))
        remote(held, held, *sems).start()
        return remote(held, coming, *sems)

    project(0)
    own_q.wait()
    pl.semaphore_wait(barrier, 22)
    spread = [z_pass(0, 0, 3), z_pass(1, 0, -3)]
    to_hub(2)
    to_hub(-2)
    project(1)
    to_hub(1)
    to_hub(-1)
    to_hub(0)
    hub2r, hub2l, far_up, hub_2r, hub_2l, far_down, hub1r, hub1l, hub_1r, hub_1l, hub0r, hub0l = stage1

    spread[0].wait()
    spread[1].wait()
    spread2 = [z_pass(2, -3, 3), z_pass(3, 3, -3)]

    halves = (slice(0, 32), slice(32, 64))

    def half_pass(i, src, dst, half, step):
        copy = remote(src.at[pl.ds(32 * half, 32), :], dst.at[pl.ds(32 * half, 32), :],
                      rs_send.at[i], rs_recv.at[i], (dp, at_z(step)))
        copy.start()
        return copy

    hub2r.wait_recv()
    hub2l.wait_recv()
    far_up.wait_recv()
    part[rel(6)] = part[rel(6)] + from_left[4] + from_right[4]
    part[rel(6), 0:32, :] = part[rel(6), 0:32, :] + eighth[0]
    up2 = [half_pass(12, part.at[rel(6)], second.at[0], 0, 3)]
    hub_2r.wait_recv()
    hub_2l.wait_recv()
    far_down.wait_recv()
    part[rel(-6)] = part[rel(-6)] + from_left[0] + from_right[0]
    part[rel(-6), 32:64, :] = part[rel(-6), 32:64, :] + eighth[1]
    down2 = [half_pass(13, part.at[rel(-6)], second.at[1], 0, -3)]
    up2.append(half_pass(14, part.at[rel(6)], second.at[0], 1, 3))
    down2.append(half_pass(15, part.at[rel(-6)], second.at[1], 1, -3))

    hub1r.wait_recv()
    hub1l.wait_recv()
    hub_1r.wait_recv()
    hub_1l.wait_recv()
    up = part[rel(3)] + from_left[3] + from_right[3]
    down = part[rel(-3)] + from_left[1] + from_right[1]
    hub0r.wait_recv()
    hub0l.wait_recv()
    mine = part[rel(0)] + from_left[2] + from_right[2]

    spread2[0].wait()
    spread2[1].wait()
    near = [z_pass(4, 6, -2)]
    for i, offset in enumerate((0, 3, -3, 6, -6)):
        near += [z_pass(5 + i, offset, 1), z_pass(10 + i, offset, -1)]

    up3, down3 = [], []
    for h, rows in enumerate(halves):
        up2[h].wait_recv()
        part[rel(3), rows, :] = up[rows] + second[0, rows, :]
        up3.append(half_pass(16 + h, part.at[rel(3)], third.at[0], h, 3))
        down2[h].wait_recv()
        part[rel(-3), rows, :] = down[rows] + second[1, rows, :]
        down3.append(half_pass(18 + h, part.at[rel(-3)], third.at[1], h, -3))

    def plane(of_core, a, b):
        x, y = lax.rem(dp // 2, 4), dp // 8
        dx = a * (1 - of_core) + b * of_core
        dy = b * (1 - of_core) + a * of_core
        return (lax.rem(y + dy + 4, 4) * 4 + lax.rem(x + dx + 4, 4)) * 2 + of_core

    def index(a, b):
        return 4 * (a % 4) + b % 4

    q_sent = []

    def q_pass(a, b, da, db):
        i = index(a - da, b - db)
        block = q_block(plane(core, a, b))
        copy = remote(block, block, qp_send.at[i], qp_recv.at[i], (plane(core, da, db), z))
        copy.start()
        q_sent.append(copy)

    def q_split(which):
        for from_z in range(16):
            block = q[from_z, q_rows(which), q_lanes(which)]
            high = block.astype(bf16)
            qhi[from_z, q_rows(which), q_lanes(which)] = high
            qlo[from_z, q_rows(which), q_lanes(which)] = (block - high.astype(f32)).astype(bf16)

    def q_mate(a, b):
        block = q_block(plane(core, a, b))
        i = index(a, b)
        copy = remote(block, block, qc_send.at[i], qc_recv.at[i], (sibling, z))
        copy.start()
        q_sent.append(copy)

    def q_take(a, b):
        i = index(a, b)
        block = q_block(plane(core, a, b))
        remote(block, block, qp_send.at[i], qp_recv.at[i], (sibling, z)).wait_recv()
        q_mate(a, b)

    def q_take_mate(a, b):
        i = index(a, b)
        which = plane(1 - core, a, b)
        remote(q_block(which), q_block(which), qc_send.at[i], qc_recv.at[i], (sibling, z)).wait_recv()
        q_split(which)

    for piece in near:
        piece.wait()
    for da, db in ((1, 0), (-1, 0), (2, 0), (0, 1), (0, -1)):
        q_pass(0, 0, da, db)
    q_mate(0, 0)
    q_split(dp)

    for copy in up3 + down3:
        copy.wait_recv()
    x = mine + third[0] + third[1]

    fin, fout = factors(dot_tn(x, x, HIGHEST))
    first_core = core == 0
    fsend[...] = jnp.where(first_core, fout, fin)
    fisher_pair = remote(fsend, fpair, f_send.at[0], f_recv.at[0], (sibling, z))
    fisher_pair.start()
    keep = jnp.where(first_core, fin, fout)
    fisher_pair.wait_recv()
    ftile[...] = keep + fpair[...]

    others = pl.ds(1, 15)
    for i in (8, 7, 9, 6, 10, 5, 11, 4, 12, 3, 13, 2, 14, 1, 15):
        remote(ftile, fz.at[i], fsum_send.at[0], fsum_recv.at[0], (dp, at_z(i))).start()

    turned = x.T
    acts_turned = jnp.concatenate([turned[0:32], turned[64:96]], axis=1)
    grads_turned = jnp.concatenate([turned[32:64], turned[96:128]], axis=1)

    for a in (1, -1, 2):
        q_take(a, 0)
        q_pass(a, 0, 0, 1)
        q_pass(a, 0, 0, -1)
    q_pass(2, 0, 0, 2)
    q_take(0, 1)
    q_pass(0, 1, 0, -1)
    q_take(0, -1)
    for a, b in ((1, 0), (-1, 0), (0, 1), (0, -1), (2, 0)):
        q_split(plane(core, a, b))
    q_take_mate(0, 0)

    def take_all(own, ref, which):
        pltpu.make_async_copy(ref.at[others], ref.at[others], fsum_recv.at[which]).wait()
        terms = [own[...]] + [ref[i] for i in range(1, 16)]
        while len(terms) > 1:
            terms = [a + b for a, b in zip(terms[::2], terms[1::2])]
        return terms[0]

    zsum[...] = take_all(ftile, fz, 0)
    for i in (10, 6, 9, 11, 5, 7, 2, 14, 8, 4, 12, 3, 13, 1, 15):
        remote(zsum, fp.at[i], fsum_send.at[1], fsum_recv.at[1], (chip(i), z)).start()

    def sent_all(ref, which):
        pltpu.make_async_copy(ref.at[others], ref.at[others], fsum_send.at[which]).wait()

    for copy in stage1 + up2 + down2 + up3 + down3 + [fisher_pair]:
        copy.wait_send()
    sent_all(fz, 0)

    for a in (1, -1):
        q_take(a, 1)
        q_pass(a, 1, 0, -1)
    for a, b in ((1, -1), (-1, -1), (0, 2), (2, 1), (2, -1)):
        q_take(a, b)
    for a, b in ((1, 1), (-1, 1), (1, -1), (-1, -1), (0, 2), (2, 1), (2, -1)):
        q_split(plane(core, a, b))
    for a, b in ((1, 0), (-1, 0), (0, 1), (0, -1), (2, 0), (1, 1), (-1, 1), (1, -1), (-1, -1), (0, 2)):
        q_take_mate(a, b)

    for copy in q_sent[:6]:
        copy.wait_send()
    fisher = unpack(take_all(zsum, fp, 1))
    eye = iota((32, 128), 0) == iota((32, 128), 1)
    fisher = fisher / tokens + jnp.where(eye, damping, 0.0)
    minv[...] = inverse(jnp.where(iota((32, 128), 1) < 32, fisher, 0.0))
    swap = remote(minv, mpair, f_send.at[1], f_recv.at[1], (sibling, z))
    swap.start()

    for a, b in ((2, 2), (1, 2), (-1, 2)):
        q_take(a, b)
        q_split(plane(core, a, b))
    for a, b in ((2, 1), (2, -1), (2, 2), (1, 2), (-1, 2)):
        q_take_mate(a, b)

    swap.wait_recv()
    mine_inv, other_inv = minv[...], mpair[...]
    inv_in = jnp.where(first_core, mine_inv, other_inv)[:, 0:32]
    inv_out = jnp.where(first_core, other_inv, mine_inv)[:, 0:32]
    acts_ready = dot_nn(inv_in, acts_turned, HIGHEST)
    grads_ready = dot_nn(inv_out, grads_turned, HIGHEST) * (1.0 / 32.0)
    for a in range(32):
        rows = slice(32 * a, 32 * a + 32)
        code = grads_ready[a : a + 1] * acts_ready
        high = code.astype(bf16)
        code_parts[rows, 0:128] = high
        code_parts[rows, 128:256] = (code - high.astype(f32)).astype(bf16)

    def score(i, carry):
        rows = pl.ds(pl.multiple_of(i * 256, 256), 256)
        four = pl.ds(4 * i, 4)
        high = qhi[four].reshape(256, 1024)
        low = qlo[four].reshape(256, 1024)
        by_high = dot_nn(high, code_parts[...])
        by_low = dot_nn(low, code_parts[:, 0:128])
        out[:, rows] = (by_high[:, 0:128] + by_high[:, 128:256] + by_low).T
        return carry

    lax.fori_loop(0, 4, score, 0)

    for copy in [swap] + q_sent[6:]:
        copy.wait_send()
    sent_all(fp, 1)


def body(hidden_acts, out_grads, proj_in, proj_out, query_codes):
    tokens = float(hidden_acts.shape[0] * lax.axis_size("dp"))
    vmem = pl.BlockSpec(memory_space=pltpu.VMEM)
    hbm = pl.BlockSpec(memory_space=pltpu.HBM)
    dma = pltpu.SemaphoreType.DMA

    def call(*refs):
        kernel(tokens, *refs)

    return pl.pallas_call(
        call,
        out_shape=pltpu.VMEM((128, 1024), f32),
        in_specs=[hbm] * 5,
        out_specs=vmem,
        scratch_shapes=[
            pltpu.VMEM((16, 128, 896), bf16),
            pltpu.VMEM((16, 128, 256), bf16),
            pltpu.VMEM((128, 2304), bf16),
            pltpu.VMEM((16, 64, 128), f32),
            pltpu.VMEM((5, 64, 128), f32),
            pltpu.VMEM((5, 64, 128), f32),
            pltpu.VMEM((2, 32, 128), f32),
            pltpu.VMEM((2, 64, 128), f32),
            pltpu.VMEM((2, 64, 128), f32),
            pltpu.VMEM((8, 128), f32),
            pltpu.VMEM((8, 128), f32),
            pltpu.VMEM((8, 128), f32),
            pltpu.VMEM((16, 8, 128), f32),
            pltpu.VMEM((8, 128), f32),
            pltpu.VMEM((16, 8, 128), f32),
            pltpu.VMEM((32, 128), f32),
            pltpu.VMEM((32, 128), f32),
            pltpu.VMEM((16, 64, 1024), f32),
            pltpu.VMEM((16, 64, 1024), bf16),
            pltpu.VMEM((16, 64, 1024), bf16),
            pltpu.VMEM((1024, 256), bf16),
            dma((4,)),
            dma((2, 2)),
            dma,
            dma((20,)), dma((20,)),
            dma((2,)), dma((2,)),
            dma((2,)), dma((2,)),
            dma((16,)), dma((16,)),
            dma((16,)), dma((16,)),
            dma((16,)), dma((16,)),
        ],
        name="influence",
        compiler_params=pltpu.CompilerParams(
            collective_id=0, has_side_effects=True, vmem_limit_bytes=24 << 20
        ),
    )(*[
        pltpu.with_memory_space_constraint(a, pltpu.HBM)
        for a in (hidden_acts, out_grads, proj_in.T, proj_out.T, query_codes)
    ])


def solution(mesh):
    return jax.shard_map(
        body,
        mesh=mesh,
        in_specs=(
            P("dp", "query"),
            P("dp", "query"),
            P("query", None),
            P("query", None),
            P("query", None),
        ),
        out_specs=P(("dp", "query"), None),
        check_vma=False,
    )
```

```python
import jax
import jax.numpy as jnp
from jax import lax
from jax.experimental import pallas as pl
from jax.experimental.pallas import tpu as pltpu
from jax.sharding import PartitionSpec as P

damping = 0.1
MESH = pl.DeviceIdType.MESH
HIGHEST = lax.Precision.HIGHEST
f32 = jnp.float32
bf16 = jnp.bfloat16


def dot_nt(a, b, precision=None):
    return lax.dot_general(
        a, b, (((1,), (1,)), ((), ())), precision=precision, preferred_element_type=f32
    )


def dot_nn(a, b, precision=None):
    return lax.dot_general(
        a, b, (((1,), (0,)), ((), ())), precision=precision, preferred_element_type=f32
    )


def dot_tn(a, b, precision=None):
    return lax.dot_general(
        a, b, (((0,), (0,)), ((), ())), precision=precision, preferred_element_type=f32
    )


def iota(shape, axis):
    return lax.broadcasted_iota(jnp.int32, shape, axis)


def factors(product):
    lane = iota((32, 128), 1) // 32

    def block(k):
        kept = jnp.where(lane == k, product[32 * k : 32 * k + 32], 0.0)
        return pltpu.roll(kept, 128 - 32 * k, 1) if k else kept

    def pack(square):
        tile = square[0:8]
        for k in range(1, 4):
            tile = tile + pltpu.roll(square[8 * k : 8 * k + 8], 32 * k, 1)
        return tile

    return pack(block(0) + block(2)), pack(block(1) + block(3))


def unpack(tile):
    rows = [tile] + [pltpu.roll(tile, 128 - 32 * k, 1) for k in range(1, 4)]
    return jnp.concatenate(rows, axis=0)


def inverse(matrix):
    lane = iota((1, 128), 1)
    row_id = iota((8, 128), 0)
    tiles = [matrix[8 * t : 8 * t + 8] for t in range(4)]
    for b in range(4):
        spread = [
            [jnp.broadcast_to(tiles[t][:, 8 * b + j : 8 * b + j + 1], (8, 128)) for t in range(4)]
            for j in range(8)
        ]
        for j in range(8):
            k = 8 * b + j
            columns = spread[j]
            pivot = 1.0 / columns[b][j : j + 1]
            row = jnp.where(lane == k, 1.0, tiles[b][j : j + 1]) * pivot
            factors_next = [columns[b][n : n + 1] * pivot for n in range(j + 1, 8)]
            columns = [jnp.where(row_id == j, -1.0, c) if t == b else c for t, c in enumerate(columns)]
            for t in range(4):
                kept = jnp.where(lane == k, 0.0, tiles[t])
                if t == b:
                    kept = jnp.where(row_id == j, 0.0, kept)
                tiles[t] = kept - columns[t] * row
            for n, factor in zip(range(j + 1, 8), factors_next):
                for t in range(4):
                    kept = spread[n][t]
                    if t == b:
                        kept = jnp.where(row_id == j, 0.0, kept)
                    spread[n][t] = kept - columns[t] * factor
    return jnp.concatenate(tiles, axis=0)


def kernel(
    tokens, hid, grd, wi, wo, codes, out,
    hbuf, gbuf, proj, part, inbox, second, third,
    fsend, fpair, ftile, fz, zsum, fp, minv, mpair, q, qhi, qlo, code_parts,
    weight_sem, load_sem, qload_sem, rs_send, rs_recv, f_send, f_recv, fsum_send, fsum_recv,
    qz_send, qz_recv, qp_send, qp_recv, qc_send, qc_recv,
):
    dp = lax.axis_index("dp")
    z = lax.axis_index("query")
    core = lax.rem(dp, 2)
    sibling = dp + 1 - 2 * core

    def at_z(offset):
        return lax.rem(z + offset + 16, 16)

    def chip(i):
        return lax.rem(dp + 2 * i, 32)

    def rel(offset):
        return (offset - 5) % 16

    def remote(src, dst, ss, rs, device):
        return pltpu.make_async_remote_copy(
            src_ref=src, dst_ref=dst, send_sem=ss, recv_sem=rs,
            device_id=device, device_id_type=MESH,
        )

    barrier = pltpu.get_barrier_semaphore()

    def hello_chip(i, carry):
        pl.semaphore_signal(barrier, inc=1, device_id=(chip(i), z), device_id_type=MESH)
        return carry

    for offset in (3, -3, 2, -2, 1, -1):
        pl.semaphore_signal(barrier, inc=1, device_id=(dp, at_z(offset)), device_id_type=MESH)
    lax.fori_loop(1, 16, hello_chip, 0)
    pl.semaphore_signal(barrier, inc=1, device_id=(sibling, z), device_id_type=MESH)

    def wait_bytes(ref, sem):
        pltpu.make_async_copy(ref, ref, sem).wait()

    weights_in = []
    for half in range(2):
        for src, start, width, at in ((wi, 0, 896, 0), (wo, 896, 256, 32)):
            rows = pl.ds(64 * half + at, 32)
            lanes = pl.ds(1152 * half + start, width)
            weights_in.append(pltpu.make_async_copy(
                src, proj.at[rows, lanes], weight_sem
            ))
    proj[...] = jnp.zeros_like(proj)
    for copy in weights_in:
        copy.start()
    loads = []
    chunks = ((0, 7), (7, 9))
    for g, (start, count) in enumerate(chunks):
        def load(j, carry, g=g):
            rows = pl.ds(pl.multiple_of(at_z(5 + j) * 128, 128), 128)
            pltpu.make_async_copy(hid.at[rows, :], hbuf.at[j], load_sem.at[g, 0]).start()
            pltpu.make_async_copy(grd.at[rows, :], gbuf.at[j], load_sem.at[g, 1]).start()
            return carry

        lax.fori_loop(start, start + count, load, 0)
        held = pl.ds(start, count)
        loads.append((
            pltpu.make_async_copy(hbuf.at[held], hbuf.at[held], load_sem.at[g, 0]),
            pltpu.make_async_copy(gbuf.at[held], gbuf.at[held], load_sem.at[g, 1]),
        ))

    def q_rows(which):
        return pl.ds(pl.multiple_of((which // 8) * 16, 16), 16)

    def q_lanes(which):
        return pl.ds(pl.multiple_of(lax.rem(which, 8) * 128, 128), 128)

    def q_piece(from_z):
        return q.at[from_z, q_rows(dp), q_lanes(dp)]

    def q_block(which):
        return q.at[:, q_rows(which), q_lanes(which)]

    own_q = pltpu.make_async_copy(codes.at[q_rows(dp), q_lanes(dp)], q_piece(z), qload_sem)
    own_q.start()

    wait_bytes(proj.at[pl.ds(0, 64), pl.ds(0, 1152)], weight_sem)

    def project(g):
        start, count = chunks[g]
        loads[g][0].wait()
        loads[g][1].wait()
        total = None
        for half in range(2):
            rows = slice(64 * half, 64 * half + 64)
            for ref, lane, width in ((hbuf, 0, 896), (gbuf, 896, 256)):
                left = ref[start : start + count, rows, :].reshape(64 * count, width)
                lane = lane + 1152 * half
                term = dot_nt(left, proj[:, lane : lane + width])
                total = term if total is None else total + term
        part[start : start + count] = total.reshape(count, 64, 128)

    def to_hub(m):
        i = m + 2
        remote(part.at[rel(3 * m + 1)], inbox.at[i, pl.ds(0, 64)],
               rs_send, rs_recv.at[i], (dp, at_z(1))).start()
        remote(part.at[rel(3 * m - 1)], inbox.at[i, pl.ds(64, 64)],
               rs_send, rs_recv.at[i], (dp, at_z(-1))).start()
        if abs(m) == 2:
            s = 0 if m == 2 else 32
            remote(part.at[rel(8), pl.ds(s, 32), :], inbox.at[i, pl.ds(128, 32)],
                   rs_send, rs_recv.at[i], (dp, at_z(m))).start()

    def hub(m):
        i = m + 2
        wait_bytes(inbox.at[i, pl.ds(0, 160 if abs(m) == 2 else 128)], rs_recv.at[i])
        return part[rel(3 * m)] + inbox[i, 0:64, :] + inbox[i, 64:128, :]

    def z_pass(i, offset, step):
        held = q_piece(at_z(offset))
        remote(held, held, qz_send, qz_recv.at[i], (dp, at_z(step))).start()

    def z_wait(i, pieces):
        wait_bytes(q.at[pl.ds(0, pieces), pl.ds(0, 16), pl.ds(0, 128)], qz_recv.at[i])

    project(0)
    own_q.wait()
    pl.semaphore_wait(barrier, 22)
    z_pass(0, 0, 3)
    z_pass(0, 0, -3)
    to_hub(2)
    to_hub(-2)
    project(1)
    to_hub(1)
    to_hub(-1)
    to_hub(0)

    z_wait(0, 2)
    z_pass(1, -3, 3)
    z_pass(1, 3, -3)

    halves = (slice(0, 32), slice(32, 64))

    def half_pass(i, src, dst, half, step):
        copy = remote(src.at[pl.ds(32 * half, 32), :], dst.at[pl.ds(32 * half, 32), :],
                      rs_send, rs_recv.at[i], (dp, at_z(step)))
        copy.start()
        return copy

    part[rel(6)] = hub(2)
    part[rel(6), 0:32, :] = part[rel(6), 0:32, :] + inbox[4, 128:160, :]
    up2 = [half_pass(5, part.at[rel(6)], second.at[0], 0, 3)]
    part[rel(-6)] = hub(-2)
    part[rel(-6), 32:64, :] = part[rel(-6), 32:64, :] + inbox[0, 128:160, :]
    down2 = [half_pass(6, part.at[rel(-6)], second.at[1], 0, -3)]
    up2.append(half_pass(7, part.at[rel(6)], second.at[0], 1, 3))
    down2.append(half_pass(8, part.at[rel(-6)], second.at[1], 1, -3))

    up, down, mine = hub(1), hub(-1), hub(0)

    z_wait(1, 2)
    z_pass(2, 6, -2)
    for offset in (0, 3, -3, 6, -6):
        z_pass(2, offset, 1)
        z_pass(2, offset, -1)

    for h, rows in enumerate(halves):
        up2[h].wait_recv()
        part[rel(3), rows, :] = up[rows] + second[0, rows, :]
        half_pass(9, part.at[rel(3)], third.at[0], h, 3)
        down2[h].wait_recv()
        part[rel(-3), rows, :] = down[rows] + second[1, rows, :]
        half_pass(9, part.at[rel(-3)], third.at[1], h, -3)

    def plane(of_core, a, b):
        x, y = lax.rem(dp // 2, 4), dp // 8
        dx = a * (1 - of_core) + b * of_core
        dy = b * (1 - of_core) + a * of_core
        return (lax.rem(y + dy + 4, 4) * 4 + lax.rem(x + dx + 4, 4)) * 2 + of_core

    def index(a, b):
        return 4 * (a % 4) + b % 4

    groups = (
        ((0, 0),),
        ((1, 0), (-1, 0), (0, 1), (0, -1), (2, 0)),
        ((1, 1), (-1, 1), (1, -1), (-1, -1), (0, 2)),
        ((2, 1), (2, -1), (2, 2), (1, 2), (-1, 2)),
    )
    group = {place: g for g, places in enumerate(groups) for place in places}

    def q_pass(a, b, da, db):
        i = index(a - da, b - db)
        block = q_block(plane(core, a, b))
        remote(block, block, qp_send, qp_recv.at[i], (plane(core, da, db), z)).start()

    def q_split(which):
        for from_z in range(16):
            block = q[from_z, q_rows(which), q_lanes(which)]
            high = block.astype(bf16)
            qhi[from_z, q_rows(which), q_lanes(which)] = high
            qlo[from_z, q_rows(which), q_lanes(which)] = (block - high.astype(f32)).astype(bf16)

    def q_mate(a, b):
        block = q_block(plane(core, a, b))
        remote(block, block, qc_send, qc_recv.at[group[a, b]], (sibling, z)).start()

    def q_take(a, b):
        i = index(a, b)
        block = q_block(plane(core, a, b))
        wait_bytes(block, qp_recv.at[i])
        q_mate(a, b)

    def q_take_mates(g):
        wait_bytes(q.at[pl.ds(0, len(groups[g])), pl.ds(0, 32), :], qc_recv.at[g])
        for a, b in groups[g]:
            q_split(plane(1 - core, a, b))

    z_wait(2, 11)
    for da, db in ((1, 0), (-1, 0), (2, 0), (0, 1), (0, -1)):
        q_pass(0, 0, da, db)
    q_mate(0, 0)
    q_split(dp)

    wait_bytes(third, rs_recv.at[9])
    x = mine + third[0] + third[1]

    fin, fout = factors(dot_tn(x, x, HIGHEST))
    first_core = core == 0
    fsend[...] = jnp.where(first_core, fout, fin)
    fisher_pair = remote(fsend, fpair, f_send.at[0], f_recv.at[0], (sibling, z))
    fisher_pair.start()
    keep = jnp.where(first_core, fin, fout)
    fisher_pair.wait_recv()
    ftile[...] = keep + fpair[...]

    others = pl.ds(1, 15)
    for i in (8, 7, 9, 6, 10, 5, 11, 4, 12, 3, 13, 2, 14, 1, 15):
        remote(ftile, fz.at[i], fsum_send.at[0], fsum_recv.at[0], (dp, at_z(i))).start()

    turned = x.T
    acts_turned = jnp.concatenate([turned[0:32], turned[64:96]], axis=1)
    grads_turned = jnp.concatenate([turned[32:64], turned[96:128]], axis=1)

    for a in (1, -1, 2):
        q_take(a, 0)
        q_pass(a, 0, 0, 1)
        q_pass(a, 0, 0, -1)
    q_pass(2, 0, 0, 2)
    q_take(0, 1)
    q_pass(0, 1, 0, -1)
    q_take(0, -1)
    for a, b in ((1, 0), (-1, 0), (0, 1), (0, -1), (2, 0)):
        q_split(plane(core, a, b))
    q_take_mates(0)

    def take_all(own, ref, which):
        pltpu.make_async_copy(ref.at[others], ref.at[others], fsum_recv.at[which]).wait()
        terms = [own[...]] + [ref[i] for i in range(1, 16)]
        while len(terms) > 1:
            terms = [a + b for a, b in zip(terms[::2], terms[1::2])]
        return terms[0]

    zsum[...] = take_all(ftile, fz, 0)
    for i in (10, 6, 9, 11, 5, 7, 2, 14, 8, 4, 12, 3, 13, 1, 15):
        remote(zsum, fp.at[i], fsum_send.at[1], fsum_recv.at[1], (chip(i), z)).start()

    def sent_all(ref, which):
        pltpu.make_async_copy(ref.at[others], ref.at[others], fsum_send.at[which]).wait()

    wait_bytes(part.at[pl.ds(0, 15)], rs_send)
    fisher_pair.wait_send()
    wait_bytes(q.at[pl.ds(0, 15), pl.ds(0, 16), pl.ds(0, 128)], qz_send)
    sent_all(fz, 0)

    for a in (1, -1):
        q_take(a, 1)
        q_pass(a, 1, 0, -1)
    for a, b in ((1, -1), (-1, -1), (0, 2), (2, 1), (2, -1)):
        q_take(a, b)
    for a, b in ((1, 1), (-1, 1), (1, -1), (-1, -1), (0, 2), (2, 1), (2, -1)):
        q_split(plane(core, a, b))
    q_take_mates(1)
    q_take_mates(2)

    fisher = unpack(take_all(zsum, fp, 1))
    eye = iota((32, 128), 0) == iota((32, 128), 1)
    fisher = fisher / tokens + jnp.where(eye, damping, 0.0)
    minv[...] = inverse(jnp.where(iota((32, 128), 1) < 32, fisher, 0.0))
    swap = remote(minv, mpair, f_send.at[1], f_recv.at[1], (sibling, z))
    swap.start()

    for a, b in ((2, 2), (1, 2), (-1, 2)):
        q_take(a, b)
        q_split(plane(core, a, b))
    q_take_mates(3)

    swap.wait_recv()
    mine_inv, other_inv = minv[...], mpair[...]
    inv_in = jnp.where(first_core, mine_inv, other_inv)[:, 0:32]
    inv_out = jnp.where(first_core, other_inv, mine_inv)[:, 0:32]
    acts_ready = dot_nn(inv_in, acts_turned, HIGHEST)
    grads_ready = dot_nn(inv_out, grads_turned, HIGHEST) * (1.0 / 32.0)
    for a in range(32):
        rows = slice(32 * a, 32 * a + 32)
        code = grads_ready[a : a + 1] * acts_ready
        high = code.astype(bf16)
        code_parts[rows, 0:128] = high
        code_parts[rows, 128:256] = (code - high.astype(f32)).astype(bf16)

    def score(i, carry):
        rows = pl.ds(pl.multiple_of(i * 256, 256), 256)
        four = pl.ds(4 * i, 4)
        high = qhi[four].reshape(256, 1024)
        low = qlo[four].reshape(256, 1024)
        by_high = dot_nn(high, code_parts[...])
        by_low = dot_nn(low, code_parts[:, 0:128])
        out[:, rows] = (by_high[:, 0:128] + by_high[:, 128:256] + by_low).T
        return carry

    lax.fori_loop(0, 4, score, 0)

    swap.wait_send()
    wait_bytes(q.at[pl.ds(0, 15), pl.ds(0, 32), :], qp_send)
    wait_bytes(q.at[:, pl.ds(0, 32), :], qc_send)
    sent_all(fp, 1)


def body(hidden_acts, out_grads, proj_in, proj_out, query_codes):
    tokens = float(hidden_acts.shape[0] * lax.axis_size("dp"))
    vmem = pl.BlockSpec(memory_space=pltpu.VMEM)
    hbm = pl.BlockSpec(memory_space=pltpu.HBM)
    dma = pltpu.SemaphoreType.DMA

    def call(*refs):
        kernel(tokens, *refs)

    return pl.pallas_call(
        call,
        out_shape=pltpu.VMEM((128, 1024), f32),
        in_specs=[hbm] * 5,
        out_specs=vmem,
        scratch_shapes=[
            pltpu.VMEM((16, 128, 896), bf16),
            pltpu.VMEM((16, 128, 256), bf16),
            pltpu.VMEM((128, 2304), bf16),
            pltpu.VMEM((16, 64, 128), f32),
            pltpu.VMEM((5, 160, 128), f32),
            pltpu.VMEM((2, 64, 128), f32),
            pltpu.VMEM((2, 64, 128), f32),
            pltpu.VMEM((8, 128), f32),
            pltpu.VMEM((8, 128), f32),
            pltpu.VMEM((8, 128), f32),
            pltpu.VMEM((16, 8, 128), f32),
            pltpu.VMEM((8, 128), f32),
            pltpu.VMEM((16, 8, 128), f32),
            pltpu.VMEM((32, 128), f32),
            pltpu.VMEM((32, 128), f32),
            pltpu.VMEM((16, 64, 1024), f32),
            pltpu.VMEM((16, 64, 1024), bf16),
            pltpu.VMEM((16, 64, 1024), bf16),
            pltpu.VMEM((1024, 256), bf16),
            dma,
            dma((2, 2)),
            dma,
            dma, dma((10,)),
            dma((2,)), dma((2,)),
            dma((2,)), dma((2,)),
            dma, dma((3,)),
            dma, dma((16,)),
            dma, dma((4,)),
        ],
        name="influence",
        compiler_params=pltpu.CompilerParams(
            collective_id=0, has_side_effects=True, vmem_limit_bytes=24 << 20
        ),
    )(*[
        pltpu.with_memory_space_constraint(a, pltpu.HBM)
        for a in (hidden_acts, out_grads, proj_in.T, proj_out.T, query_codes)
    ])


def solution(mesh):
    return jax.shard_map(
        body,
        mesh=mesh,
        in_specs=(
            P("dp", "query"),
            P("dp", "query"),
            P("query", None),
            P("query", None),
            P("query", None),
        ),
        out_specs=P(("dp", "query"), None),
        check_vma=False,
    )
```

```python
import jax
import jax.numpy as jnp
from jax import lax
from jax.experimental import pallas as pl
from jax.experimental.pallas import tpu as pltpu
from jax.sharding import PartitionSpec as P

damping = 0.1
MESH = pl.DeviceIdType.MESH
HIGHEST = lax.Precision.HIGHEST
f32 = jnp.float32
bf16 = jnp.bfloat16


def dot_nt(a, b, precision=None):
    return lax.dot_general(
        a, b, (((1,), (1,)), ((), ())), precision=precision, preferred_element_type=f32
    )


def dot_nn(a, b, precision=None):
    return lax.dot_general(
        a, b, (((1,), (0,)), ((), ())), precision=precision, preferred_element_type=f32
    )


def dot_tn(a, b, precision=None):
    return lax.dot_general(
        a, b, (((0,), (0,)), ((), ())), precision=precision, preferred_element_type=f32
    )


def iota(shape, axis):
    return lax.broadcasted_iota(jnp.int32, shape, axis)


def factors(product):
    lane = iota((32, 128), 1) // 32

    def block(k):
        kept = jnp.where(lane == k, product[32 * k : 32 * k + 32], 0.0)
        return pltpu.roll(kept, 128 - 32 * k, 1) if k else kept

    def pack(square):
        tile = square[0:8]
        for k in range(1, 4):
            tile = tile + pltpu.roll(square[8 * k : 8 * k + 8], 32 * k, 1)
        return tile

    return pack(block(0) + block(2)), pack(block(1) + block(3))


def unpack(tile):
    rows = [tile] + [pltpu.roll(tile, 128 - 32 * k, 1) for k in range(1, 4)]
    return jnp.concatenate(rows, axis=0)


def inverse(matrix):
    lane = iota((1, 128), 1)
    row_id = iota((8, 128), 0)
    tiles = [matrix[8 * t : 8 * t + 8] for t in range(4)]
    for b in range(4):
        spread = [
            [jnp.broadcast_to(tiles[t][:, 8 * b + j : 8 * b + j + 1], (8, 128)) for t in range(4)]
            for j in range(8)
        ]
        for j in range(8):
            k = 8 * b + j
            columns = spread[j]
            pivot = 1.0 / columns[b][j : j + 1]
            row = jnp.where(lane == k, 1.0, tiles[b][j : j + 1]) * pivot
            factors_next = [columns[b][n : n + 1] * pivot for n in range(j + 1, 8)]
            columns = [jnp.where(row_id == j, -1.0, c) if t == b else c for t, c in enumerate(columns)]
            for t in range(4):
                kept = jnp.where(lane == k, 0.0, tiles[t])
                if t == b:
                    kept = jnp.where(row_id == j, 0.0, kept)
                tiles[t] = kept - columns[t] * row
            for n, factor in zip(range(j + 1, 8), factors_next):
                for t in range(4):
                    kept = spread[n][t]
                    if t == b:
                        kept = jnp.where(row_id == j, 0.0, kept)
                    spread[n][t] = kept - columns[t] * factor
    return jnp.concatenate(tiles, axis=0)


def kernel(
    tokens, hid, grd, wi, wo, codes, out,
    hbuf, gbuf, proj, part, inbox, second, third,
    fsend, fpair, ftile, fz, zsum, fp, minv, mpair, q, qhi, qlo, code_parts,
    weight_sem, load_sem, qload_sem, rs_send, rs_recv, f_send, f_recv, fsum_send, fsum_recv,
    qz_send, qz_recv, qp_send, qp_recv, qc_send, qc_recv,
):
    dp = lax.axis_index("dp")
    z = lax.axis_index("query")
    core = lax.rem(dp, 2)
    sibling = dp + 1 - 2 * core

    def at_z(offset):
        return lax.rem(z + offset + 16, 16)

    def chip(i):
        return lax.rem(dp + 2 * i, 32)

    def rel(offset):
        return (offset - 5) % 16

    def remote(src, dst, ss, rs, device):
        return pltpu.make_async_remote_copy(
            src_ref=src, dst_ref=dst, send_sem=ss, recv_sem=rs,
            device_id=device, device_id_type=MESH,
        )

    def wait_bytes(ref, sem):
        pltpu.make_async_copy(ref, ref, sem).wait()

    barrier = pltpu.get_barrier_semaphore()

    for offset in (3, -3, 2, -2, 1, -1):
        pl.semaphore_signal(barrier, inc=1, device_id=(dp, at_z(offset)), device_id_type=MESH)
    for i in (10, 6, 9, 11, 5, 7, 2, 14, 8, 4, 12, 3, 13, 1, 15):
        pl.semaphore_signal(barrier, inc=1, device_id=(chip(i), z), device_id_type=MESH)
    pl.semaphore_signal(barrier, inc=1, device_id=(sibling, z), device_id_type=MESH)

    loads = []
    chunks = ((0, 7), (7, 9))
    def start_loads(g):
        start, count = chunks[g]

        def load(j, carry):
            rows = pl.ds(pl.multiple_of(at_z(5 + j) * 128, 128), 128)
            pltpu.make_async_copy(hid.at[rows, :], hbuf.at[j], load_sem.at[g, 0]).start()
            pltpu.make_async_copy(grd.at[rows, :], gbuf.at[j], load_sem.at[g, 1]).start()
            return carry

        lax.fori_loop(start, start + count, load, 0)
        held = pl.ds(start, count)
        loads.append((
            pltpu.make_async_copy(hbuf.at[held], hbuf.at[held], load_sem.at[g, 0]),
            pltpu.make_async_copy(gbuf.at[held], gbuf.at[held], load_sem.at[g, 1]),
        ))

    start_loads(0)
    weights_in = []
    for half in range(2):
        for src, start, width, at in ((wi, 0, 896, 0), (wo, 896, 256, 32)):
            rows = pl.ds(64 * half + at, 32)
            lanes = pl.ds(1152 * half + start, width)
            weights_in.append(pltpu.make_async_copy(
                src, proj.at[rows, lanes], weight_sem
            ))
    proj[...] = jnp.zeros_like(proj)
    for copy in weights_in:
        copy.start()
    start_loads(1)

    def q_rows(which):
        return pl.ds(pl.multiple_of((which // 8) * 16, 16), 16)

    def q_lanes(which):
        return pl.ds(pl.multiple_of(lax.rem(which, 8) * 128, 128), 128)

    def q_piece(from_z):
        return q.at[from_z, q_rows(dp), q_lanes(dp)]

    def q_block(which):
        return q.at[:, q_rows(which), q_lanes(which)]

    own_q = pltpu.make_async_copy(codes.at[q_rows(dp), q_lanes(dp)], q_piece(z), qload_sem)
    own_q.start()

    wait_bytes(proj.at[pl.ds(0, 64), pl.ds(0, 1152)], weight_sem)

    def project(g):
        start, count = chunks[g]
        loads[g][0].wait()
        loads[g][1].wait()
        total = None
        for half in range(2):
            rows = slice(64 * half, 64 * half + 64)
            for ref, lane, width in ((hbuf, 0, 896), (gbuf, 896, 256)):
                left = ref[start : start + count, rows, :].reshape(64 * count, width)
                lane = lane + 1152 * half
                term = dot_nt(left, proj[:, lane : lane + width])
                total = term if total is None else total + term
        part[start : start + count] = total.reshape(count, 64, 128)

    def to_hub(m):
        i = m + 2
        remote(part.at[rel(3 * m + 1)], inbox.at[i, pl.ds(0, 64)],
               rs_send, rs_recv.at[i], (dp, at_z(1))).start()
        remote(part.at[rel(3 * m - 1)], inbox.at[i, pl.ds(64, 64)],
               rs_send, rs_recv.at[i], (dp, at_z(-1))).start()
        if abs(m) == 2:
            s = 0 if m == 2 else 32
            remote(part.at[rel(8), pl.ds(s, 32), :], inbox.at[i, pl.ds(128, 32)],
                   rs_send, rs_recv.at[i], (dp, at_z(m))).start()

    def hub(m):
        i = m + 2
        wait_bytes(inbox.at[i, pl.ds(0, 160 if abs(m) == 2 else 128)], rs_recv.at[i])
        return part[rel(3 * m)] + inbox[i, 0:64, :] + inbox[i, 64:128, :]

    def z_pass(i, offset, step):
        held = q_piece(at_z(offset))
        remote(held, held, qz_send, qz_recv.at[i], (dp, at_z(step))).start()

    def z_wait(i, pieces):
        wait_bytes(q.at[pl.ds(0, pieces), pl.ds(0, 16), pl.ds(0, 128)], qz_recv.at[i])

    project(0)
    own_q.wait()
    pl.semaphore_wait(barrier, 22)
    z_pass(0, 0, 3)
    z_pass(0, 0, -3)
    to_hub(2)
    to_hub(-2)
    project(1)
    to_hub(1)
    to_hub(-1)
    to_hub(0)

    z_wait(0, 2)
    z_pass(1, -3, 3)
    z_pass(1, 3, -3)

    halves = (slice(0, 32), slice(32, 64))

    def half_pass(i, src, dst, half, step):
        copy = remote(src.at[pl.ds(32 * half, 32), :], dst.at[pl.ds(32 * half, 32), :],
                      rs_send, rs_recv.at[i], (dp, at_z(step)))
        copy.start()
        return copy

    part[rel(6)] = hub(2)
    part[rel(6), 0:32, :] = part[rel(6), 0:32, :] + inbox[4, 128:160, :]
    up2 = [half_pass(5, part.at[rel(6)], second.at[0], 0, 3)]
    part[rel(-6)] = hub(-2)
    part[rel(-6), 32:64, :] = part[rel(-6), 32:64, :] + inbox[0, 128:160, :]
    down2 = [half_pass(6, part.at[rel(-6)], second.at[1], 0, -3)]
    up2.append(half_pass(7, part.at[rel(6)], second.at[0], 1, 3))
    down2.append(half_pass(8, part.at[rel(-6)], second.at[1], 1, -3))

    up, down, mine = hub(1), hub(-1), hub(0)

    z_wait(1, 2)
    z_pass(2, 6, -2)
    for offset in (0, 3, -3, 6, -6):
        z_pass(2, offset, 1)
        z_pass(2, offset, -1)

    for h, rows in enumerate(halves):
        up2[h].wait_recv()
        part[rel(3), rows, :] = up[rows] + second[0, rows, :]
        half_pass(9, part.at[rel(3)], third.at[0], h, 3)
        down2[h].wait_recv()
        part[rel(-3), rows, :] = down[rows] + second[1, rows, :]
        half_pass(9, part.at[rel(-3)], third.at[1], h, -3)

    def plane(of_core, a, b):
        x, y = lax.rem(dp // 2, 4), dp // 8
        dx = a * (1 - of_core) + b * of_core
        dy = b * (1 - of_core) + a * of_core
        return (lax.rem(y + dy + 4, 4) * 4 + lax.rem(x + dx + 4, 4)) * 2 + of_core

    def index(a, b):
        return 4 * (a % 4) + b % 4

    groups = (
        ((0, 0),),
        ((1, 0), (-1, 0), (0, 1), (0, -1), (2, 0)),
        ((1, 1), (-1, 1), (1, -1), (-1, -1), (0, 2)),
        ((2, 1), (2, -1), (2, 2), (1, 2), (-1, 2)),
    )
    group = {place: g for g, places in enumerate(groups) for place in places}

    def q_pass(a, b, da, db):
        i = index(a - da, b - db)
        block = q_block(plane(core, a, b))
        remote(block, block, qp_send, qp_recv.at[i], (plane(core, da, db), z)).start()

    def q_split(which):
        for from_z in range(16):
            block = q[from_z, q_rows(which), q_lanes(which)]
            high = block.astype(bf16)
            qhi[from_z, q_rows(which), q_lanes(which)] = high
            qlo[from_z, q_rows(which), q_lanes(which)] = (block - high.astype(f32)).astype(bf16)

    def q_mate(a, b):
        block = q_block(plane(core, a, b))
        remote(block, block, qc_send, qc_recv.at[group[a, b]], (sibling, z)).start()

    def q_take(a, b):
        i = index(a, b)
        block = q_block(plane(core, a, b))
        wait_bytes(block, qp_recv.at[i])
        q_mate(a, b)

    def q_take_mates(g):
        wait_bytes(q.at[pl.ds(0, len(groups[g])), pl.ds(0, 32), :], qc_recv.at[g])
        for a, b in groups[g]:
            q_split(plane(1 - core, a, b))

    z_wait(2, 11)
    for da, db in ((1, 0), (-1, 0), (2, 0), (0, 1), (0, -1)):
        q_pass(0, 0, da, db)
    q_mate(0, 0)
    q_split(dp)

    wait_bytes(third, rs_recv.at[9])
    x = mine + third[0] + third[1]

    fin, fout = factors(dot_tn(x, x, HIGHEST))
    first_core = core == 0
    fsend[...] = jnp.where(first_core, fout, fin)
    fisher_pair = remote(fsend, fpair, f_send.at[0], f_recv.at[0], (sibling, z))
    fisher_pair.start()
    keep = jnp.where(first_core, fin, fout)
    fisher_pair.wait_recv()
    ftile[...] = keep + fpair[...]

    others = pl.ds(1, 15)
    for i in (8, 7, 9, 6, 10, 5, 11, 4, 12, 3, 13, 2, 14, 1, 15):
        remote(ftile, fz.at[i], fsum_send.at[0], fsum_recv.at[0], (dp, at_z(i))).start()

    turned = x.T
    acts_turned = jnp.concatenate([turned[0:32], turned[64:96]], axis=1)
    grads_turned = jnp.concatenate([turned[32:64], turned[96:128]], axis=1)

    for a in (1, -1, 2):
        q_take(a, 0)
        q_pass(a, 0, 0, 1)
        q_pass(a, 0, 0, -1)
    q_pass(2, 0, 0, 2)
    q_take(0, 1)
    q_pass(0, 1, 0, -1)
    q_take(0, -1)
    for a, b in ((1, 0), (-1, 0), (0, 1), (0, -1), (2, 0)):
        q_split(plane(core, a, b))
    q_take_mates(0)

    def take_all(own, ref, which):
        pltpu.make_async_copy(ref.at[others], ref.at[others], fsum_recv.at[which]).wait()
        terms = [own[...]] + [ref[i] for i in range(1, 16)]
        while len(terms) > 1:
            terms = [a + b for a, b in zip(terms[::2], terms[1::2])]
        return terms[0]

    zsum[...] = take_all(ftile, fz, 0)
    for i in (10, 6, 9, 11, 5, 7, 2, 14, 8, 4, 12, 3, 13, 1, 15):
        remote(zsum, fp.at[i], fsum_send.at[1], fsum_recv.at[1], (chip(i), z)).start()

    def sent_all(ref, which):
        pltpu.make_async_copy(ref.at[others], ref.at[others], fsum_send.at[which]).wait()

    wait_bytes(part.at[pl.ds(0, 15)], rs_send)
    fisher_pair.wait_send()
    wait_bytes(q.at[pl.ds(0, 15), pl.ds(0, 16), pl.ds(0, 128)], qz_send)
    sent_all(fz, 0)

    for a in (1, -1):
        q_take(a, 1)
        q_pass(a, 1, 0, -1)
    for a, b in ((1, -1), (-1, -1), (0, 2), (2, 1), (2, -1)):
        q_take(a, b)
    for a, b in ((1, 1), (-1, 1), (1, -1), (-1, -1), (0, 2), (2, 1), (2, -1)):
        q_split(plane(core, a, b))
    q_take_mates(1)
    q_take_mates(2)

    fisher = unpack(take_all(zsum, fp, 1))
    eye = iota((32, 128), 0) == iota((32, 128), 1)
    fisher = fisher / tokens + jnp.where(eye, damping, 0.0)
    minv[...] = inverse(jnp.where(iota((32, 128), 1) < 32, fisher, 0.0))
    swap = remote(minv, mpair, f_send.at[1], f_recv.at[1], (sibling, z))
    swap.start()

    for a, b in ((2, 2), (1, 2), (-1, 2)):
        q_take(a, b)
        q_split(plane(core, a, b))
    q_take_mates(3)

    swap.wait_recv()
    mine_inv, other_inv = minv[...], mpair[...]
    inv_in = jnp.where(first_core, mine_inv, other_inv)[:, 0:32]
    inv_out = jnp.where(first_core, other_inv, mine_inv)[:, 0:32]
    acts_ready = dot_nn(inv_in, acts_turned, HIGHEST)
    grads_ready = dot_nn(inv_out, grads_turned, HIGHEST) * (1.0 / 32.0)
    for a in range(32):
        rows = slice(32 * a, 32 * a + 32)
        code = grads_ready[a : a + 1] * acts_ready
        high = code.astype(bf16)
        code_parts[rows, 0:128] = high
        code_parts[rows, 128:256] = (code - high.astype(f32)).astype(bf16)

    def score(i, carry):
        rows = pl.ds(pl.multiple_of(i * 256, 256), 256)
        four = pl.ds(4 * i, 4)
        high = qhi[four].reshape(256, 1024)
        low = qlo[four].reshape(256, 1024)
        by_high = dot_nn(high, code_parts[...])
        by_low = dot_nn(low, code_parts[:, 0:128])
        out[:, rows] = (by_high[:, 0:128] + by_high[:, 128:256] + by_low).T
        return carry

    lax.fori_loop(0, 4, score, 0)

    swap.wait_send()
    wait_bytes(q.at[pl.ds(0, 15), pl.ds(0, 32), :], qp_send)
    wait_bytes(q.at[:, pl.ds(0, 32), :], qc_send)
    sent_all(fp, 1)


def body(hidden_acts, out_grads, proj_in, proj_out, query_codes):
    tokens = float(hidden_acts.shape[0] * lax.axis_size("dp"))
    vmem = pl.BlockSpec(memory_space=pltpu.VMEM)
    hbm = pl.BlockSpec(memory_space=pltpu.HBM)
    dma = pltpu.SemaphoreType.DMA

    def call(*refs):
        kernel(tokens, *refs)

    return pl.pallas_call(
        call,
        out_shape=pltpu.VMEM((128, 1024), f32),
        in_specs=[hbm] * 5,
        out_specs=vmem,
        scratch_shapes=[
            pltpu.VMEM((16, 128, 896), bf16),
            pltpu.VMEM((16, 128, 256), bf16),
            pltpu.VMEM((128, 2304), bf16),
            pltpu.VMEM((16, 64, 128), f32),
            pltpu.VMEM((5, 160, 128), f32),
            pltpu.VMEM((2, 64, 128), f32),
            pltpu.VMEM((2, 64, 128), f32),
            pltpu.VMEM((8, 128), f32),
            pltpu.VMEM((8, 128), f32),
            pltpu.VMEM((8, 128), f32),
            pltpu.VMEM((16, 8, 128), f32),
            pltpu.VMEM((8, 128), f32),
            pltpu.VMEM((16, 8, 128), f32),
            pltpu.VMEM((32, 128), f32),
            pltpu.VMEM((32, 128), f32),
            pltpu.VMEM((16, 64, 1024), f32),
            pltpu.VMEM((16, 64, 1024), bf16),
            pltpu.VMEM((16, 64, 1024), bf16),
            pltpu.VMEM((1024, 256), bf16),
            dma,
            dma((2, 2)),
            dma,
            dma, dma((10,)),
            dma((2,)), dma((2,)),
            dma((2,)), dma((2,)),
            dma, dma((3,)),
            dma, dma((16,)),
            dma, dma((4,)),
        ],
        name="influence",
        compiler_params=pltpu.CompilerParams(
            collective_id=0, has_side_effects=True, vmem_limit_bytes=24 << 20
        ),
    )(*[
        pltpu.with_memory_space_constraint(a, pltpu.HBM)
        for a in (hidden_acts, out_grads, proj_in.T, proj_out.T, query_codes)
    ])


def solution(mesh):
    return jax.shard_map(
        body,
        mesh=mesh,
        in_specs=(
            P("dp", "query"),
            P("dp", "query"),
            P("query", None),
            P("query", None),
            P("query", None),
        ),
        out_specs=P(("dp", "query"), None),
        check_vma=False,
    )
```
